128 devices in a mesh: pre: 16 (over y, z), dec: 8 (over x, core).
Axes of the slice: x: 4, y: 4, z: 4, core: 2. Of those that a mesh axis runs over, the one named last changes fastest.
Arguments:
- hidden: bfloat16 [8, 6144, 7168], P('dec', None, 'pre'), may hold values from -6 to 6
- kv_down: bfloat16 [7168, 576], P('pre'), may hold values from -0.0625 to 0.0625
- kv_gain: float32 [512], replicated, may hold values from 0.1 to 1.9
- uk_weight: bfloat16 [128, 128, 512], P('pre'), may hold values from -0.5 to 0.5
- uv_weight: bfloat16 [128, 512, 128], P('pre'), may hold values from -0.25 to 0.25
- queries: bfloat16 [8, 16, 4, 128, 192], P('dec', None, None, 'pre'), may hold values from -100 to 100
- new_keys: bfloat16 [8, 16, 4, 576], P('dec'), may hold values from -6 to 6
- lengths: int32 [8, 16], replicated, may hold values from 1 to 384, 3840 in all within a row
- assign: int32 [128], replicated, may hold values from 0 to 127, each once
- block_table: int32 [8, 96], P('dec'), may hold values from 0 to 95, each once within a row
Outputs:
- cache: bfloat16 [8, 6144, 576], P('dec', 'pre')
- attended: bfloat16 [8, 16, 4, 128, 128], P('dec', None, None, 'pre')
The draws below stay inside these ranges and needn't reach their ends.
Inputs may be any that keep to these rules, and one draw needn't show every extreme that they name: `lengths`: span d holds 16 request slots of 384 tokens; row d sums to 3840 and some request of each span fills its slot. Request r = d * 16 + j is the one in slot j of span d; decode slot b of instance e serves request assign[e * 16 + b]; every request is served once. `block_table`: each row is a permutation of the pages of one decode instance.
All inputs are finite; a program needn't handle non-finite values.
Results may differ from the reference program's by a relative error of at most 0.0082.
Values may be sent and summed in bfloat16 or wider, within the bound.
No kernel may reach another device: no remote copies, remote signals or barrier semaphores. Data moves between devices by JAX's collectives and lax.ppermute only.
A program may use at most 128 MiB of HBM per device.

```python
import math
import jax
import jax.numpy as jnp
import numpy as np
from jax import lax

D = 7168
LAT = 512
ROPE = 64
HEADS = 128
HDIM = 128
VDIM = 128
TOK_DEV = 384
BLK = 64
STEPS = 4
REQS = 16
PRE_TOK = 6144
NPG = 6
PAGES = 96
N_DEC = 8


def draw_queries(key, part):
    base_key = jax.random.fold_in(key, 11)
    extent = (N_DEC, REQS, STEPS, HEADS, HDIM + ROPE)
    return jnp.clip(jax.random.normal(base_key, extent, jnp.float32), -6.0, 6.0).astype(jnp.bfloat16)


def draw_new_keys(key, part):
    base_key = jax.random.fold_in(key, 23)
    extent = (N_DEC, REQS, STEPS, LAT + ROPE)
    return jnp.clip(jax.random.normal(base_key, extent, jnp.float32), -6.0, 6.0).astype(jnp.bfloat16)


def steps_of(rng, dims, cuts, smallest, largest):
    def one(dim, blocks):
        draws = jax.random.uniform(jax.random.fold_in(jax.random.fold_in(rng, 6), dim), (blocks,), jnp.float32, smallest / len(cuts), largest / len(cuts))
        return jnp.repeat(jnp.exp(draws), dims[dim] // blocks).reshape((-1,) + (1,) * (len(dims) - dim - 1))

    gain = one(*cuts[0])
    for cut in cuts[1:]:
        gain = gain * one(*cut)
    return gain


def length_profile(count, total, limit, lean):
    weights = [(1 << 20) // math.isqrt(rank ** lean) + 1 for rank in range(2, count + 1)]
    rest, given = total - limit - (count - 1), [1] * (count - 1)
    while rest > 0:
        movable = [i for i in range(count - 1) if given[i] < limit]
        mass, left = sum([weights[i] for i in movable]), rest
        for i in movable:
            more = min(limit - given[i], max(1, left * weights[i] // mass), rest)
            given[i] = given[i] + more
            rest = rest - more
    return np.array([limit] + given)


def uneven(key, amount, total, reach, skew):
    if amount == 2:
        one = jax.random.randint(key, (), max(1, total - reach), min(reach, total - 1) + 1)
        return jnp.stack([one, total - one])
    sizes = jnp.asarray(length_profile(amount, total, reach, skew), jnp.int32)
    couples = (amount - 1) // 2
    source_of, sink = sizes[1:1 + 2 * couples:2], sizes[2:2 + 2 * couples:2]
    margin = jnp.minimum(source_of - 1, reach - sink)
    passed = jax.random.randint(jax.random.fold_in(key, 1), (couples,), 0, 1 << 20) % (margin + 1)
    sizes = sizes.at[1:1 + 2 * couples:2].set(source_of - passed).at[2:2 + 2 * couples:2].set(sink + passed)
    return sizes[jax.random.permutation(jax.random.fold_in(key, 2), amount)]


def normal_values(rng, dims, deviation, limit, pieces=(), kind=jnp.bfloat16):
    values = jax.random.normal(rng, dims, jnp.float32) * deviation
    if len(pieces) > 0:
        values = steps_of(rng, dims, pieces, -0.22, 0.18) * values
    return jnp.clip(values, min=-limit, max=limit).astype(kind)


def setup_inputs(seed: int = 0) -> dict:
    key_list = jax.random.split(jax.random.key(seed), 11)
    return {
        "hidden": normal_values(key_list[0], (N_DEC, PRE_TOK, D), 1.0, 6.0, ((0, 8), (2, 16))),
        "kv_down": normal_values(key_list[1], (D, LAT + ROPE), D ** -0.5, 0.0625, ((0, 16),)),
        "kv_gain": jnp.clip(1.0 + 0.18 * jax.random.normal(key_list[2], (LAT,), jnp.float32), 0.1, 1.9),
        "uk_weight": normal_values(key_list[3], (HEADS, HDIM, LAT), HDIM ** -0.5, 0.5, ((0, 16),)),
        "uv_weight": normal_values(key_list[4], (HEADS, LAT, VDIM), LAT ** -0.5, 0.25, ((0, 16),)),
        "queries": draw_queries(jax.random.fold_in(key_list[10], 71), 0),
        "new_keys": draw_new_keys(jax.random.fold_in(key_list[10], 71), 0),
        "lengths": jax.vmap(lambda own: uneven(own, REQS, 5 * PRE_TOK // 8, TOK_DEV, 2))(jax.random.split(key_list[7], N_DEC)).reshape((N_DEC, REQS)).astype(jnp.int32),
        "assign": jax.random.permutation(key_list[8], N_DEC * REQS).astype(jnp.int32),
        "block_table": jax.vmap(lambda own: jax.random.permutation(own, PAGES))(jax.random.split(key_list[9], N_DEC)).reshape((N_DEC, PAGES)).astype(jnp.int32),
    }


EPS = 1e-06

def rotate(values, positions):
    half_rope = ROPE // 2
    frequency = 10000.0 ** (-jnp.arange(half_rope, dtype=jnp.float32) * 2.0 / ROPE)
    angles = positions[:, None].astype(jnp.float32) * frequency[None, :]
    cosine, sine_part = (jnp.cos(angles), jnp.sin(angles))
    first_half, second_half = (values[..., :half_rope], values[..., half_rope:])
    return jnp.concatenate([first_half * cosine - second_half * sine_part, second_half * cosine + first_half * sine_part], -1)

def reference(hidden, kv_down, kv_gain, uk_weight, uv_weight, queries, new_keys, lengths, assign, block_table):
    row_width = LAT + ROPE
    positions = jnp.tile(jnp.arange(TOK_DEV, dtype=jnp.int32), REQS)

    def compress(span_rows):
        projected = jnp.dot(span_rows, kv_down, preferred_element_type=jnp.float32)
        latent = projected[:, :LAT]
        scaling = lax.rsqrt(lax.optimization_barrier(jnp.mean(latent * latent, -1, keepdims=True)) + EPS)
        latent_part = (latent * scaling * kv_gain).astype(jnp.bfloat16)
        rope_part = rotate(projected[:, LAT:], positions).astype(jnp.bfloat16)
        return jnp.concatenate([latent_part, rope_part], -1)
    slots = lax.map(compress, hidden).reshape(N_DEC * REQS, TOK_DEV, row_width)
    flat_lengths = lengths.reshape(-1)
    live_rows = jnp.arange(TOK_DEV, dtype=jnp.int32)[None, :] < flat_lengths[:, None]
    slots = jnp.where(live_rows[:, :, None], slots, jnp.zeros((), jnp.bfloat16))
    ordered = slots[assign].reshape(N_DEC, REQS * NPG, BLK, row_width)

    def place(table_row, blocks):
        return jnp.zeros((PAGES, BLK, row_width), jnp.bfloat16).at[table_row].set(blocks)
    cache = jax.vmap(place)(block_table, ordered)
    page_table = block_table.reshape(N_DEC, REQS, NPG)
    keys = jax.vmap(lambda pages_all, table_part: pages_all[table_part])(cache, page_table)
    keys = keys.reshape(N_DEC, REQS, TOK_DEV, row_width)
    slot_lengths = flat_lengths[assign].reshape(N_DEC, REQS)
    absorbed = jnp.einsum('ebshk,hkl->ebshl', queries[..., :HDIM].astype(jnp.float32), uk_weight.astype(jnp.float32)).astype(jnp.bfloat16)
    query_full = jnp.concatenate([absorbed, queries[..., HDIM:]], -1).astype(jnp.float32)
    score_scale = 1.0 / math.sqrt(HDIM + ROPE)
    cache_scores = jnp.einsum('ebshc,ebtc->ebsht', query_full, keys.astype(jnp.float32)) * score_scale
    fresh_scores = jnp.einsum('ebshc,ebtc->ebsht', query_full, new_keys.astype(jnp.float32)) * score_scale
    cache_live = (jnp.arange(TOK_DEV, dtype=jnp.int32)[None, None, :] < slot_lengths[:, :, None])[:, :, None, None, :]
    fresh_live = (jnp.arange(STEPS)[None, :] <= jnp.arange(STEPS)[:, None])[None, None, :, None, :]
    cache_scores = jnp.where(cache_live, cache_scores, -1e+30)
    fresh_scores = jnp.where(fresh_live, fresh_scores, -1e+30)
    top_score = jnp.maximum(lax.optimization_barrier(jnp.max(cache_scores, -1)), lax.optimization_barrier(jnp.max(fresh_scores, -1)))[..., None]
    cache_exp = jnp.exp(cache_scores - top_score)
    fresh_exp = jnp.exp(fresh_scores - top_score)
    denominator = lax.optimization_barrier(jnp.sum(cache_exp, -1, keepdims=True)) + lax.optimization_barrier(jnp.sum(fresh_exp, -1, keepdims=True))
    cache_prob = (cache_exp / denominator).astype(jnp.bfloat16)
    fresh_prob = (fresh_exp / denominator).astype(jnp.bfloat16)
    mixed = jnp.einsum('ebsht,ebtl->ebshl', cache_prob.astype(jnp.float32), keys[..., :LAT].astype(jnp.float32))
    mixed = mixed + jnp.einsum('ebsht,ebtl->ebshl', fresh_prob.astype(jnp.float32), new_keys[..., :LAT].astype(jnp.float32))
    mixed = mixed.astype(jnp.bfloat16)
    attended = jnp.einsum('ebshl,hlv->ebshv', mixed.astype(jnp.float32), uv_weight.astype(jnp.float32)).astype(jnp.bfloat16)
    return (cache.reshape(N_DEC, PAGES * BLK, row_width), attended)
```

```python
import functools
import math

import jax
import jax.numpy as jnp
from jax import lax
from jax.experimental import pallas as pl
from jax.experimental.pallas import tpu as pltpu
from jax.sharding import PartitionSpec as P

LAT = 512
ROPE = 64
WIDTH = LAT + ROPE
HDIM = 128
BLK = 64
TOK = 384
REQS = 16
RUN = TOK // REQS
NPG = TOK // BLK
PACK = 256
HOLD = 288
WINDOW = 32
SIDE = 4
STEPS = 4

EPS = 1e-06
BF = jnp.bfloat16
F32 = jnp.float32


def project_kernel(len_ref, hid_ref, down_ref, out_ref, shift_ref, hold_ref, start_ref):
    step = pl.program_id(0)

    @pl.when(step == 0)
    def _():
        start_ref[0] = 0
        hold_ref[...] = jnp.zeros_like(hold_ref)
        shape = (REQS, WINDOW, TOK)
        offset = lax.broadcasted_iota(jnp.int32, shape, 2)
        offset = offset - lax.broadcasted_iota(jnp.int32, shape, 0)
        shift_ref[...] = offset - REQS * lax.broadcasted_iota(jnp.int32, shape, 1)

    start = start_ref[0]
    count = lax.div(len_ref[step] + (REQS - 1), REQS)
    lead = lax.rem(start, 8)
    base = pl.multiple_of(start - lead, 8)

    for tile in range(1, TOK // 128 + 1):
        tokens, window = 128 * tile, 8 * tile + 8

        @pl.when((count > 8 * tile - 8) & (count <= 8 * tile))
        def _():
            hid = hid_ref[:, :tokens]
            token = lax.broadcasted_iota(jnp.int32, hid.shape, 1)
            hid = jnp.where(token < count * REQS, hid, jnp.zeros((), BF))
            chosen = jnp.where(shift_ref[:, :window, :tokens] == -REQS * lead, 1.0, 0.0)
            chosen = chosen.reshape(REQS * window, tokens).astype(BF)
            rows = lax.dot_general(
                chosen, hid, (((1,), (1,)), ((), ())), preferred_element_type=F32
            ).astype(BF)
            part = jnp.dot(rows, down_ref[...], preferred_element_type=F32)
            hold_ref[:, pl.ds(base, window), :] += part.reshape(REQS, window, WIDTH)

    start_ref[0] = start + count

    @pl.when(step == pl.num_programs(0) - 1)
    def _():
        out_ref[...] = hold_ref[:, :PACK, :].astype(BF)


def project(lengths_row, hidden_t, kv_down):
    depth = hidden_t.shape[0]
    return pl.pallas_call(
        project_kernel,
        out_shape=jax.ShapeDtypeStruct((REQS, PACK, WIDTH), BF),
        grid_spec=pltpu.PrefetchScalarGridSpec(
            num_scalar_prefetch=1,
            grid=(REQS,),
            in_specs=[
                pl.BlockSpec((depth, TOK), lambda r, _: (0, r)),
                pl.BlockSpec((depth, WIDTH), lambda r, _: (0, 0)),
            ],
            out_specs=pl.BlockSpec((REQS, PACK, WIDTH), lambda r, _: (0, 0, 0)),
            scratch_shapes=[
                pltpu.VMEM((REQS, WINDOW, TOK), jnp.int32),
                pltpu.VMEM((REQS, HOLD, WIDTH), F32),
                pltpu.SMEM((1,), jnp.int32),
            ],
        ),
        compiler_params=pltpu.CompilerParams(vmem_limit_bytes=48 << 20),
        cost_estimate=pl.CostEstimate(
            flops=2 * REQS * TOK * depth * WIDTH, bytes_accessed=11 << 20, transcendentals=0
        ),
    )(lengths_row, hidden_t, kv_down)


def attend_kernel(query_ref, keys_ref, fresh_ref, live_ref, out_ref):
    rows = query_ref.shape[0]
    query = query_ref[...]
    keys = keys_ref[...]
    fresh = fresh_ref[...]
    scale = 1.0 / math.sqrt(HDIM + ROPE)
    across = (((1,), (1,)), ((), ()))
    score = lax.dot_general(query, keys, across, preferred_element_type=F32) * scale
    score = jnp.where(live_ref[...] > 0, score, -1e30)
    later = lax.dot_general(query, fresh, across, preferred_element_type=F32) * scale
    row = lax.broadcasted_iota(jnp.int32, later.shape, 0)
    column = lax.broadcasted_iota(jnp.int32, later.shape, 1)
    at_step = lax.rem(lax.div(row, 8), STEPS)
    later = jnp.where(column <= at_step, later, -1e30)
    top = jnp.maximum(jnp.max(score, -1, keepdims=True), jnp.max(later, -1, keepdims=True))
    score = jnp.exp(score - top)
    later = jnp.exp(later - top)
    total = jnp.sum(score, -1, keepdims=True) + jnp.sum(later, -1, keepdims=True)
    score = (score / total).astype(BF)
    later = (later / total).astype(BF)
    mixed = jnp.dot(score, keys[:, :LAT], preferred_element_type=F32)
    mixed = mixed + jnp.dot(later, fresh[:, :LAT], preferred_element_type=F32)
    out_ref[...] = mixed.astype(BF)


def attend(query, keys, fresh, live):
    count, block = query.shape[0], 128
    return pl.pallas_call(
        attend_kernel,
        out_shape=jax.ShapeDtypeStruct((count, LAT), BF),
        grid=(count // block,),
        in_specs=[
            pl.BlockSpec((block, WIDTH), lambda i: (i, 0)),
            pl.BlockSpec(keys.shape, lambda i: (0, 0)),
            pl.BlockSpec(fresh.shape, lambda i: (0, 0)),
            pl.BlockSpec(live.shape, lambda i: (0, 0)),
        ],
        out_specs=pl.BlockSpec((block, LAT), lambda i: (i, 0)),
        compiler_params=pltpu.CompilerParams(vmem_limit_bytes=24 << 20),
    )(query, keys, fresh, live)


def pick(index, values):
    ids = jnp.arange(values.shape[0], dtype=jnp.int32)
    return jnp.sum(jnp.where(index[..., None] == ids, values, 0), -1)


def groups_of(sides, first):
    found = []
    for core in range(2):
        for x in range(SIDE):
            for other in range(SIDE):
                ring = []
                for k in range(SIDE):
                    y, z = (k, other) if core == first else (other, k)
                    ring.append(((y * SIDE + z) * SIDE + x) * 2 + core)
                found.append(ring)
    return found


def shards(
    hidden, kv_down, kv_gain, uk_weight, uv_weight, queries, new_keys, lengths, assign, block_table
):
    pre_rank = lax.axis_index("pre")
    dec_rank = lax.axis_index("dec")
    both = ("pre", "dec")
    side_y, side_z = pre_rank // SIDE, pre_rank % SIDE
    swapped = side_z * SIDE + side_y
    residue = jnp.where(dec_rank % 2 == 0, pre_rank, swapped)

    counts = (lengths + (REQS - 1)) // REQS
    ends = jnp.cumsum(counts, 1)
    starts = ends - counts
    own_lengths = lax.dynamic_index_in_dim(lengths, dec_rank, 0, keepdims=False)
    own_starts = lax.dynamic_index_in_dim(starts, dec_rank, 0, keepdims=False)
    own_ends = lax.dynamic_index_in_dim(ends, dec_rank, 0, keepdims=False)

    packed = project(own_lengths, hidden[0].T, kv_down)

    packed = packed.reshape(SIDE, SIDE, PACK, WIDTH)
    packed = lax.all_to_all(packed, both, 0, 0, tiled=True, axis_index_groups=groups_of(SIDE, 0))
    packed = jnp.sum(packed.astype(F32), 0).astype(BF)
    packed = lax.all_to_all(packed, both, 0, 0, tiled=True, axis_index_groups=groups_of(SIDE, 1))
    projected = jnp.sum(packed.astype(F32), 0)

    row = jnp.arange(PACK, dtype=jnp.int32)
    inside = (row[:, None] >= own_starts) & (row[:, None] < own_ends)
    place = jnp.sum(jnp.where(inside, row[:, None] - own_starts, 0), 1)
    limit = jnp.sum(jnp.where(inside, own_lengths, 0), 1)
    position = place * REQS + residue
    valid = (position < limit)[:, None]
    half = ROPE // 2
    frequency = 10000.0 ** (-jnp.arange(half, dtype=F32) * 2.0 / ROPE)
    angles = position[:, None].astype(F32) * frequency[None, :]
    cosine, sine = jnp.cos(angles), jnp.sin(angles)
    projected = jnp.where(valid, projected, 0.0)
    latent = projected[:, :LAT]
    scaling = lax.rsqrt(jnp.mean(latent * latent, -1, keepdims=True) + EPS)
    first, second = projected[:, LAT : LAT + half], projected[:, LAT + half :]
    rows = jnp.concatenate(
        [
            latent * scaling * kv_gain,
            first * cosine - second * sine,
            second * cosine + first * sine,
        ],
        -1,
    ).astype(BF)

    local_queries = queries[0]
    absorbed = jnp.einsum(
        "bshk,hkl->bshl", local_queries[..., :HDIM], uk_weight, preferred_element_type=F32
    ).astype(BF)
    query_full = jnp.concatenate([absorbed, local_queries[..., HDIM:]], -1)
    query_full = query_full.reshape(REQS, -1, WIDTH)
    rows, query_full = lax.optimization_barrier((rows, query_full))
    everything = lax.all_gather(rows, "dec", axis=0, tiled=True)
    query_full = lax.all_to_all(query_full, "pre", 0, 0, tiled=True)

    slots = lax.dynamic_slice_in_dim(assign, dec_rank * REQS, REQS)
    slot_start = pick(slots, (starts + jnp.arange(starts.shape[0])[:, None] * PACK).reshape(-1))
    slot_count = pick(slots, counts.reshape(-1))
    slot_length = pick(slots, lengths.reshape(-1))
    slot_odd = (slots // REQS) % 2
    run = jnp.arange(RUN, dtype=jnp.int32)
    by_slot = jnp.where(run < slot_count[:, None], slot_start[:, None] + run, -1)
    table = block_table[0]
    pages = table.shape[0]
    page = jnp.arange(pages, dtype=jnp.int32)
    block = jnp.sum(jnp.where(table[None, :] == page[:, None], page[None, :], 0), 1)
    owner, part = block // NPG, block % NPG
    piece = part[:, None] * (RUN // NPG) + jnp.arange(RUN // NPG, dtype=jnp.int32)
    by_page = jnp.where(
        piece < pick(owner, slot_count)[:, None], pick(owner, slot_start)[:, None] + piece, -1
    )
    source = jnp.concatenate([by_slot, by_page.reshape(REQS, RUN)], 1).reshape(-1)
    selector = (source[:, None] == jnp.arange(everything.shape[0], dtype=jnp.int32)).astype(BF)
    outgoing = jnp.dot(selector, everything, preferred_element_type=F32).astype(BF)
    outgoing = outgoing.reshape(REQS, 2 * RUN, WIDTH)
    arrived = lax.all_to_all(outgoing, "pre", 0, 0, tiled=True)

    sender = jnp.arange(REQS, dtype=jnp.int32)
    sender_swapped = (sender % SIDE) * SIDE + sender // SIDE
    page_odd = pick(owner, slot_odd).reshape(REQS, NPG)
    page_odd = lax.dynamic_index_in_dim(page_odd, pre_rank, 0, keepdims=False)
    sent_residue = jnp.where(page_odd[None, :] == 0, sender[:, None], sender_swapped[:, None])
    target = (
        jnp.arange(NPG, dtype=jnp.int32)[None, :, None] * BLK
        + jnp.arange(RUN // NPG, dtype=jnp.int32)[None, None, :] * REQS
        + sent_residue[:, :, None]
    ).reshape(-1)
    to_place = (jnp.arange(TOK, dtype=jnp.int32)[:, None] == target[None, :]).astype(BF)
    cache = jnp.dot(
        to_place, arrived[:, RUN:].reshape(TOK, WIDTH), preferred_element_type=F32
    ).astype(BF)

    own_odd = lax.dynamic_index_in_dim(slot_odd, pre_rank, 0, keepdims=False)
    own_length = lax.dynamic_index_in_dim(slot_length, pre_rank, 0, keepdims=False)
    key_residue = jnp.where(own_odd == 0, sender, sender_swapped)
    key_position = run[None, :] * REQS + key_residue[:, None]
    live = (key_position < own_length).astype(jnp.int32).reshape(1, TOK)
    fresh = lax.dynamic_index_in_dim(new_keys[0], pre_rank, 0, keepdims=False)
    fresh = jnp.pad(fresh, ((0, 16 - STEPS), (0, 0)))
    mixed = attend(
        query_full.reshape(-1, WIDTH), arrived[:, :RUN].reshape(TOK, WIDTH), fresh, live
    )
    mixed = lax.all_to_all(mixed.reshape(REQS, -1, LAT), "pre", 0, 0, tiled=True)
    mixed = mixed.reshape(REQS, STEPS, -1, LAT)
    attended = jnp.einsum("bshl,hlv->bshv", mixed, uv_weight, preferred_element_type=F32).astype(BF)
    return (cache[None], attended[None])


def solution(mesh):
    return jax.shard_map(
        shards,
        mesh=mesh,
        in_specs=(
            P("dec", None, "pre"),
            P("pre", None),
            P(),
            P("pre", None, None),
            P("pre", None, None),
            P("dec", None, None, "pre", None),
            P("dec", None, None, None),
            P(),
            P(),
            P("dec", None),
        ),
        out_specs=(P("dec", "pre", None), P("dec", None, None, "pre", None)),
        check_vma=False,
    )
```

```python
import functools
import math

import jax
import jax.numpy as jnp
from jax import lax
from jax.experimental import pallas as pl
from jax.experimental.pallas import tpu as pltpu
from jax.sharding import PartitionSpec as P

LAT = 512
ROPE = 64
WIDTH = LAT + ROPE
HDIM = 128
BLK = 64
TOK = 384
REQS = 16
RUN = TOK // REQS
NPG = TOK // BLK
PACK = 256
HOLD = 288
WINDOW = 32
PAIR = 2
SIDE = 4
STEPS = 4

EPS = 1e-06
BF = jnp.bfloat16
F32 = jnp.float32


def project_kernel(
    own_ref, len_ref, hid_ref, down_ref, out_ref, kept_ref, shift_ref, turned_ref, hold_ref, start_ref
):
    step = pl.program_id(0)
    packs = REQS // PAIR

    @pl.when(step == 0)
    def _():
        start_ref[0] = 0
        hold_ref[...] = jnp.zeros_like(hold_ref)
        turned_ref[...] = down_ref[...].astype(F32).T.astype(BF)
        shape = (REQS, WINDOW, TOK)
        offset = lax.broadcasted_iota(jnp.int32, shape, 2)
        offset = offset - lax.broadcasted_iota(jnp.int32, shape, 0)
        shift_ref[...] = offset - REQS * lax.broadcasted_iota(jnp.int32, shape, 1)

    @pl.when(step < packs)
    def _():
        for item in range(PAIR):
            start = start_ref[0]
            length = len_ref[lax.axis_index("dec"), step * PAIR + item]
            count = lax.div(length + (REQS - 1), REQS)
            lead = lax.rem(start, 8)
            base = pl.multiple_of(start - lead, 8)

            for tile in range(1, TOK // 128 + 1):
                tokens, window = 128 * tile, 8 * tile + 8

                @pl.when((count > 8 * tile - 8) & (count <= 8 * tile))
                def _():
                    hid = hid_ref[:, item * TOK : item * TOK + tokens]
                    token = lax.broadcasted_iota(jnp.int32, hid.shape, 1)
                    hid = jnp.where(token < count * REQS, hid, jnp.zeros((), BF))
                    chosen = jnp.where(shift_ref[:, :window, :tokens] == -REQS * lead, 1.0, 0.0)
                    chosen = chosen.reshape(REQS * window, tokens).astype(BF)
                    rows = lax.dot_general(
                        chosen, hid, (((1,), (1,)), ((), ())), preferred_element_type=F32
                    )
                    hold_ref[:, pl.ds(base, window), :] += rows.reshape(REQS, window, -1)

            start_ref[0] = start + count

    @pl.when(step >= packs)
    def _():
        target = step - packs
        for item in range(SIDE):
            rows = hold_ref[target * SIDE + item, :PACK, :].astype(BF)
            part = lax.dot_general(
                turned_ref[...], rows, (((1,), (1,)), ((), ())), preferred_element_type=F32
            )
            out_ref[0, item] = part.astype(BF)

            @pl.when(target == own_ref[0])
            def _():
                kept_ref[item] = part


def project(own, lengths, hidden_t, kv_down):
    depth = hidden_t.shape[0]
    packs = REQS // PAIR
    return pl.pallas_call(
        project_kernel,
        out_shape=(
            jax.ShapeDtypeStruct((SIDE, SIDE, WIDTH, PACK), BF),
            jax.ShapeDtypeStruct((SIDE, WIDTH, PACK), F32),
        ),
        grid_spec=pltpu.PrefetchScalarGridSpec(
            num_scalar_prefetch=2,
            grid=(packs + SIDE,),
            in_specs=[
                pl.BlockSpec((depth, PAIR * TOK), lambda i, *_: (0, jnp.minimum(i, packs - 1))),
                pl.BlockSpec((depth, WIDTH), lambda i, *_: (0, 0)),
            ],
            out_specs=(
                pl.BlockSpec(
                    (1, SIDE, WIDTH, PACK), lambda i, *_: (jnp.maximum(i - packs, 0), 0, 0, 0)
                ),
                pl.BlockSpec((SIDE, WIDTH, PACK), lambda i, *_: (0, 0, 0)),
            ),
            scratch_shapes=[
                pltpu.VMEM((REQS, WINDOW, TOK), jnp.int32),
                pltpu.VMEM((WIDTH, depth), BF),
                pltpu.VMEM((REQS, HOLD, depth), F32),
                pltpu.SMEM((1,), jnp.int32),
            ],
        ),
        compiler_params=pltpu.CompilerParams(vmem_limit_bytes=58 << 20),
        cost_estimate=pl.CostEstimate(
            flops=2 * REQS * TOK * depth * WIDTH, bytes_accessed=13 << 20, transcendentals=0
        ),
    )(own, lengths, hidden_t, kv_down)


def add_up(own, kept, parts):
    total = kept
    for k in range(SIDE):
        total = total + jnp.where(own == k, 0.0, parts[k].astype(F32))
    return total


def first_sum_kernel(own_ref, parts_ref, kept_ref, out_ref, kept_out_ref):
    total = add_up(own_ref[0], kept_ref[0], parts_ref[:, 0])
    out_ref[0] = total.astype(BF)

    @pl.when(pl.program_id(0) == own_ref[1])
    def _():
        kept_out_ref[...] = total


def first_sum(own, parts, kept):
    return pl.pallas_call(
        first_sum_kernel,
        out_shape=(
            jax.ShapeDtypeStruct((SIDE, WIDTH, PACK), BF),
            jax.ShapeDtypeStruct((WIDTH, PACK), F32),
        ),
        grid_spec=pltpu.PrefetchScalarGridSpec(
            num_scalar_prefetch=1,
            grid=(SIDE,),
            in_specs=[
                pl.BlockSpec((SIDE, 1, WIDTH, PACK), lambda i, _: (0, i, 0, 0)),
                pl.BlockSpec((1, WIDTH, PACK), lambda i, _: (i, 0, 0)),
            ],
            out_specs=(
                pl.BlockSpec((1, WIDTH, PACK), lambda i, _: (i, 0, 0)),
                pl.BlockSpec((WIDTH, PACK), lambda i, _: (0, 0)),
            ),
        ),
        compiler_params=pltpu.CompilerParams(vmem_limit_bytes=58 << 20),
    )(own, parts, kept)


def finish_kernel(own_ref, parts_ref, kept_ref, gain_ref, cosine_ref, sine_ref, valid_ref, out_ref):
    half = ROPE // 2
    valid = valid_ref[...] > 0
    total = add_up(own_ref[1], kept_ref[...], parts_ref)
    total = jnp.where(valid, total, 0.0)
    latent = total[:LAT]
    scaling = lax.rsqrt(jnp.sum(latent * latent, 0, keepdims=True) / LAT + EPS)
    out_ref[:LAT] = (latent * scaling * gain_ref[...]).astype(BF)
    first, second = total[LAT : LAT + half], total[LAT + half :]
    cosine, sine = cosine_ref[...], sine_ref[...]
    out_ref[LAT : LAT + half] = (first * cosine - second * sine).astype(BF)
    out_ref[LAT + half :] = (second * cosine + first * sine).astype(BF)


def finish(own, parts, kept, gain, cosine, sine, valid):
    return pl.pallas_call(
        finish_kernel,
        out_shape=jax.ShapeDtypeStruct((WIDTH, PACK), BF),
        in_specs=[pl.BlockSpec(memory_space=pltpu.SMEM)]
        + [pl.BlockSpec(memory_space=pltpu.VMEM)] * 6,
        out_specs=pl.BlockSpec(memory_space=pltpu.VMEM),
        compiler_params=pltpu.CompilerParams(vmem_limit_bytes=24 << 20),
    )(own, parts, kept, gain, cosine, sine, valid)


def select_kernel(source_ref, order_ref, rows_ref, out_ref):
    count = rows_ref.shape[1]
    row = lax.broadcasted_iota(jnp.int32, (count, TOK), 0)
    chosen = jnp.where(row == source_ref[...], 1.0, 0.0).astype(BF)
    mine = jnp.dot(rows_ref[...], chosen, preferred_element_type=F32).astype(BF)
    column = lax.broadcasted_iota(jnp.int32, (2 * TOK, TOK), 1)
    order = jnp.where(column == order_ref[...], 1.0, 0.0).astype(BF)
    out_ref[...] = lax.dot_general(
        order, mine, (((1,), (1,)), ((), ())), preferred_element_type=F32
    ).astype(BF)


def select(source, order, rows):
    return pl.pallas_call(
        select_kernel,
        out_shape=jax.ShapeDtypeStruct((2 * TOK, WIDTH), BF),
        compiler_params=pltpu.CompilerParams(vmem_limit_bytes=40 << 20),
    )(source, order, rows)


def attend_kernel(query_ref, keys_ref, fresh_ref, live_ref, out_ref):
    rows = query_ref.shape[0]
    query = query_ref[...]
    keys = keys_ref[...]
    fresh = fresh_ref[...]
    scale = 1.0 / math.sqrt(HDIM + ROPE)
    across = (((1,), (1,)), ((), ()))
    score = lax.dot_general(query, keys, across, preferred_element_type=F32) * scale
    score = jnp.where(live_ref[...] > 0, score, -1e30)
    later = lax.dot_general(query, fresh, across, preferred_element_type=F32) * scale
    row = lax.broadcasted_iota(jnp.int32, later.shape, 0)
    column = lax.broadcasted_iota(jnp.int32, later.shape, 1)
    at_step = lax.rem(lax.div(row, 8), STEPS)
    later = jnp.where(column <= at_step, later, -1e30)
    top = jnp.maximum(jnp.max(score, -1, keepdims=True), jnp.max(later, -1, keepdims=True))
    score = jnp.exp(score - top)
    later = jnp.exp(later - top)
    total = jnp.sum(score, -1, keepdims=True) + jnp.sum(later, -1, keepdims=True)
    score = (score / total).astype(BF)
    later = (later / total).astype(BF)
    mixed = jnp.dot(score, keys[:, :LAT], preferred_element_type=F32)
    mixed = mixed + jnp.dot(later, fresh[:, :LAT], preferred_element_type=F32)
    out_ref[...] = mixed.astype(BF)


def attend(query, keys, fresh, live):
    count, block = query.shape[0], 128
    return pl.pallas_call(
        attend_kernel,
        out_shape=jax.ShapeDtypeStruct((count, LAT), BF),
        grid=(count // block,),
        in_specs=[
            pl.BlockSpec((block, WIDTH), lambda i: (i, 0)),
            pl.BlockSpec(keys.shape, lambda i: (0, 0)),
            pl.BlockSpec(fresh.shape, lambda i: (0, 0)),
            pl.BlockSpec(live.shape, lambda i: (0, 0)),
        ],
        out_specs=pl.BlockSpec((block, LAT), lambda i: (i, 0)),
        compiler_params=pltpu.CompilerParams(vmem_limit_bytes=24 << 20),
    )(query, keys, fresh, live)


def pick(index, values):
    ids = jnp.arange(values.shape[0], dtype=jnp.int32)
    return jnp.sum(jnp.where(index[..., None] == ids, values, 0), -1)


def groups_of(first):
    found = []
    for core in range(2):
        for x in range(SIDE):
            for other in range(SIDE):
                ring = []
                for k in range(SIDE):
                    y, z = (k, other) if core == first else (other, k)
                    ring.append(((y * SIDE + z) * SIDE + x) * 2 + core)
                found.append(ring)
    return found


def shards(
    hidden, kv_down, kv_gain, uk_weight, uv_weight, queries, new_keys, lengths, assign, block_table
):
    pre_rank = lax.axis_index("pre")
    dec_rank = lax.axis_index("dec")
    both = ("pre", "dec")
    side_y, side_z = pre_rank // SIDE, pre_rank % SIDE
    swapped = side_z * SIDE + side_y
    residue = jnp.where(dec_rank % 2 == 0, pre_rank, swapped)

    counts = (lengths + (REQS - 1)) // REQS
    ends = jnp.cumsum(counts, 1)
    starts = ends - counts
    own_lengths = lax.dynamic_index_in_dim(lengths, dec_rank, 0, keepdims=False)
    own_starts = lax.dynamic_index_in_dim(starts, dec_rank, 0, keepdims=False)
    own_ends = lax.dynamic_index_in_dim(ends, dec_rank, 0, keepdims=False)

    even = dec_rank % 2 == 0
    own = jnp.stack([jnp.where(even, side_y, side_z), jnp.where(even, side_z, side_y)])
    packed, kept = project(own, lengths, hidden[0].T, kv_down)

    packed = lax.all_to_all(packed, both, 0, 0, tiled=True, axis_index_groups=groups_of(0))
    packed, kept = first_sum(own, packed, kept)
    packed = lax.all_to_all(packed, both, 0, 0, tiled=True, axis_index_groups=groups_of(1))

    row = jnp.arange(PACK, dtype=jnp.int32)
    inside = (row >= own_starts[:, None]) & (row < own_ends[:, None])
    place = jnp.sum(jnp.where(inside, row - own_starts[:, None], 0), 0)
    limit = jnp.sum(jnp.where(inside, own_lengths[:, None], 0), 0)
    position = place * REQS + residue
    valid = (position < limit).astype(jnp.int32)[None, :]
    half = ROPE // 2
    frequency = 10000.0 ** (-jnp.arange(half, dtype=F32) * 2.0 / ROPE)
    angles = position[None, :].astype(F32) * frequency[:, None]
    rows = finish(own, packed, kept, kv_gain[:, None], jnp.cos(angles), jnp.sin(angles), valid)

    local_queries = queries[0]
    absorbed = jnp.einsum(
        "bshk,hkl->bshl", local_queries[..., :HDIM], uk_weight, preferred_element_type=F32
    ).astype(BF)
    query_full = jnp.concatenate([absorbed, local_queries[..., HDIM:]], -1)
    query_full = query_full.reshape(REQS, -1, WIDTH)
    rows, query_full = lax.optimization_barrier((rows, query_full))
    everything = lax.all_gather(rows, "dec", axis=1, tiled=True)
    query_full = lax.all_to_all(query_full, "pre", 0, 0, tiled=True)
    everything, query_full = lax.optimization_barrier((everything, query_full))

    slots = lax.dynamic_slice_in_dim(assign, dec_rank * REQS, REQS)
    slot_start = pick(slots, (starts + jnp.arange(starts.shape[0])[:, None] * PACK).reshape(-1))
    slot_count = pick(slots, counts.reshape(-1))
    slot_length = pick(slots, lengths.reshape(-1))
    slot_odd = (slots // REQS) % 2
    run = jnp.arange(RUN, dtype=jnp.int32)
    by_slot = jnp.where(run < slot_count[:, None], slot_start[:, None] + run, -1)
    table = block_table[0]
    pages = table.shape[0]
    page = jnp.arange(pages, dtype=jnp.int32)
    block = jnp.sum(jnp.where(table[None, :] == page[:, None], page[None, :], 0), 1)
    owner, part = block // NPG, block % NPG
    piece = part[:, None] * (RUN // NPG) + jnp.arange(RUN // NPG, dtype=jnp.int32)
    by_page = (owner[:, None] * RUN + piece).reshape(REQS, RUN)
    in_order = jnp.arange(TOK, dtype=jnp.int32).reshape(REQS, RUN)
    order = jnp.concatenate([in_order, by_page], 1).reshape(-1, 1)
    outgoing = select(by_slot.reshape(1, -1), order, everything).reshape(REQS, 2 * RUN, WIDTH)
    arrived = lax.all_to_all(outgoing, "pre", 0, 0, tiled=True)

    sender = jnp.arange(REQS, dtype=jnp.int32)
    sender_swapped = (sender % SIDE) * SIDE + sender // SIDE
    page_odd = pick(owner, slot_odd).reshape(REQS, NPG)
    page_odd = lax.dynamic_index_in_dim(page_odd, pre_rank, 0, keepdims=False)
    sent_residue = jnp.where(page_odd[None, :] == 0, sender[:, None], sender_swapped[:, None])
    target = (
        jnp.arange(NPG, dtype=jnp.int32)[None, :, None] * BLK
        + jnp.arange(RUN // NPG, dtype=jnp.int32)[None, None, :] * REQS
        + sent_residue[:, :, None]
    ).reshape(REQS, RUN)
    target = jnp.concatenate([jnp.full((REQS, RUN), -1, jnp.int32), target], 1).reshape(-1)
    to_place = (jnp.arange(TOK, dtype=jnp.int32)[:, None] == target[None, :]).astype(BF)
    arrived = arrived.reshape(2 * TOK, WIDTH)
    cache = jnp.dot(to_place, arrived, preferred_element_type=F32).astype(BF)

    own_odd = lax.dynamic_index_in_dim(slot_odd, pre_rank, 0, keepdims=False)
    own_length = lax.dynamic_index_in_dim(slot_length, pre_rank, 0, keepdims=False)
    key_residue = jnp.where(own_odd == 0, sender, sender_swapped)
    key_position = run[None, :] * REQS + key_residue[:, None]
    live = (key_position < own_length).astype(jnp.int32)
    live = jnp.concatenate([live, jnp.zeros_like(live)], 1).reshape(1, 2 * TOK)
    fresh = lax.dynamic_index_in_dim(new_keys[0], pre_rank, 0, keepdims=False)
    fresh = jnp.pad(fresh, ((0, 16 - STEPS), (0, 0)))
    mixed = attend(query_full.reshape(-1, WIDTH), arrived, fresh, live)
    mixed = lax.all_to_all(mixed.reshape(REQS, -1, LAT), "pre", 0, 0, tiled=True)
    mixed = mixed.reshape(REQS, STEPS, -1, LAT)
    attended = jnp.einsum("bshl,hlv->bshv", mixed, uv_weight, preferred_element_type=F32).astype(BF)
    return (cache[None], attended[None])


def solution(mesh):
    return jax.shard_map(
        shards,
        mesh=mesh,
        in_specs=(
            P("dec", None, "pre"),
            P("pre", None),
            P(),
            P("pre", None, None),
            P("pre", None, None),
            P("dec", None, None, "pre", None),
            P("dec", None, None, None),
            P(),
            P(),
            P("dec", None),
        ),
        out_specs=(P("dec", "pre", None), P("dec", None, None, "pre", None)),
        check_vma=False,
    )
```

```python
import functools
import math

import jax
import jax.numpy as jnp
from jax import lax
from jax.experimental import pallas as pl
from jax.experimental.pallas import tpu as pltpu
from jax.sharding import PartitionSpec as P

LAT = 512
ROPE = 64
WIDTH = LAT + ROPE
HDIM = 128
BLK = 64
TOK = 384
REQS = 16
RUN = TOK // REQS
NPG = TOK // BLK
PACK = 256
HOLD = 288
AHEAD = 3
PAIR = 2
SIDE = 4
STEPS = 4

EPS = 1e-06
BF = jnp.bfloat16
F32 = jnp.float32


def project_kernel(
    len_ref, hid_ref, down_ref, out_ref, span_ref, sent_ref, shift_ref, turned_ref, hold_ref, in_sem, out_sem
):
    def load(part):
        where = pl.ds(part * PAIR * TOK, PAIR * TOK)
        return pltpu.make_async_copy(hid_ref.at[:, where], span_ref.at[:, where], in_sem.at[part])

    def store(residue):
        where = residue // SIDE, residue % SIDE
        return pltpu.make_async_copy(sent_ref.at[residue], out_ref.at[where], out_sem.at[residue])

    parts = REQS // PAIR
    for part in range(AHEAD):
        load(part).start()
    hold_ref[...] = jnp.zeros_like(hold_ref)
    turned_ref[...] = down_ref[...].astype(F32).T.astype(BF)
    shape = (REQS, 24, 256)
    offset = lax.broadcasted_iota(jnp.int32, shape, 2)
    offset = offset - lax.broadcasted_iota(jnp.int32, shape, 0)
    shift_ref[...] = offset - REQS * lax.broadcasted_iota(jnp.int32, shape, 1)

    start = 0
    for request in range(REQS):
        part = request // PAIR
        if request % PAIR == 0:
            load(part).wait()
            if part + AHEAD < parts:
                load(part + AHEAD).start()
        length = len_ref[lax.axis_index("dec"), request]
        count = lax.div(length + (REQS - 1), REQS)
        lead = lax.rem(start, 8)
        base = pl.multiple_of(start - lead, 8)

        for first, tokens, window in ((0, 256, 24), (256, 128, 16)):
            begin = request * TOK + first
            hid = span_ref[:, begin : begin + tokens]
            token = lax.broadcasted_iota(jnp.int32, hid.shape, 1)
            hid = jnp.where(token < count * REQS - first, hid, jnp.zeros((), BF))
            chosen = jnp.where(shift_ref[:, :window, :tokens] == -REQS * lead, 1.0, 0.0)
            chosen = chosen.reshape(REQS * window, tokens).astype(BF)
            rows = lax.dot_general(
                chosen, hid, (((1,), (1,)), ((), ())), preferred_element_type=F32
            )
            place = pl.ds(pl.multiple_of(base + first // REQS, 8), window)
            hold_ref[:, place, :] += rows.reshape(REQS, window, -1)

        start = start + count

    for residue in range(REQS):
        rows = hold_ref[residue, :PACK, :].astype(BF)
        sent_ref[residue] = lax.dot_general(
            turned_ref[...], rows, (((1,), (1,)), ((), ())), preferred_element_type=F32
        ).astype(BF)
        store(residue).start()
    for residue in range(REQS):
        store(residue).wait()


def project(lengths, hidden_t, kv_down):
    depth = hidden_t.shape[0]
    return pl.pallas_call(
        project_kernel,
        out_shape=jax.ShapeDtypeStruct((SIDE, SIDE, WIDTH, PACK), BF),
        in_specs=[
            pl.BlockSpec(memory_space=pltpu.SMEM),
            pl.BlockSpec(memory_space=pl.ANY),
            pl.BlockSpec(memory_space=pltpu.VMEM),
        ],
        out_specs=pl.BlockSpec(memory_space=pl.ANY),
        scratch_shapes=[
            pltpu.VMEM((depth, REQS * TOK), BF),
            pltpu.VMEM((REQS, WIDTH, PACK), BF),
            pltpu.VMEM((REQS, 24, 256), jnp.int32),
            pltpu.VMEM((WIDTH, depth), BF),
            pltpu.VMEM((REQS, HOLD, depth), F32),
            pltpu.SemaphoreType.DMA((REQS // PAIR,)),
            pltpu.SemaphoreType.DMA((REQS,)),
        ],
        compiler_params=pltpu.CompilerParams(vmem_limit_bytes=58 << 20),
        cost_estimate=pl.CostEstimate(
            flops=2 * REQS * TOK * depth * WIDTH, bytes_accessed=11 << 20, transcendentals=0
        ),
    )(lengths, hidden_t, kv_down)


def add_up(parts):
    total = parts[0].astype(F32)
    for k in range(1, SIDE):
        total = total + parts[k].astype(F32)
    return total


def first_sum_kernel(parts_ref, out_ref, sent_ref, out_sem):
    def store(part):
        return pltpu.make_async_copy(sent_ref.at[part], out_ref.at[part], out_sem.at[part])

    for part in range(SIDE):
        sent_ref[part] = add_up(parts_ref[:, part]).astype(BF)
        store(part).start()
    for part in range(SIDE):
        store(part).wait()


def first_sum(parts):
    return pl.pallas_call(
        first_sum_kernel,
        out_shape=jax.ShapeDtypeStruct((SIDE, WIDTH, PACK), BF),
        in_specs=[pl.BlockSpec(memory_space=pltpu.VMEM)],
        out_specs=pl.BlockSpec(memory_space=pl.ANY),
        scratch_shapes=[
            pltpu.VMEM((SIDE, WIDTH, PACK), BF),
            pltpu.SemaphoreType.DMA((SIDE,)),
        ],
        compiler_params=pltpu.CompilerParams(vmem_limit_bytes=16 << 20),
    )(parts)


def finish_kernel(parts_ref, gain_ref, cosine_ref, sine_ref, valid_ref, out_ref):
    half = ROPE // 2
    valid = valid_ref[...] > 0
    total = jnp.where(valid, add_up(parts_ref), 0.0)
    latent = total[:LAT]
    scaling = lax.rsqrt(jnp.sum(latent * latent, 0, keepdims=True) / LAT + EPS)
    out_ref[:LAT] = (latent * scaling * gain_ref[...]).astype(BF)
    first, second = total[LAT : LAT + half], total[LAT + half :]
    cosine, sine = cosine_ref[...], sine_ref[...]
    out_ref[LAT : LAT + half] = (first * cosine - second * sine).astype(BF)
    out_ref[LAT + half :] = (second * cosine + first * sine).astype(BF)


def finish(parts, gain, cosine, sine, valid):
    return pl.pallas_call(
        finish_kernel,
        out_shape=jax.ShapeDtypeStruct((WIDTH, PACK), BF),
        compiler_params=pltpu.CompilerParams(vmem_limit_bytes=24 << 20),
    )(parts, gain, cosine, sine, valid)


def select_kernel(source_ref, order_ref, rows_ref, out_ref):
    count = rows_ref.shape[1]
    row = lax.broadcasted_iota(jnp.int32, (count, TOK), 0)
    chosen = jnp.where(row == source_ref[...], 1.0, 0.0).astype(BF)
    mine = jnp.dot(rows_ref[...], chosen, preferred_element_type=F32).astype(BF)
    column = lax.broadcasted_iota(jnp.int32, (2 * TOK, TOK), 1)
    order = jnp.where(column == order_ref[...], 1.0, 0.0).astype(BF)
    out_ref[...] = lax.dot_general(
        order, mine, (((1,), (1,)), ((), ())), preferred_element_type=F32
    ).astype(BF)


def select(source, order, rows):
    return pl.pallas_call(
        select_kernel,
        out_shape=jax.ShapeDtypeStruct((2 * TOK, WIDTH), BF),
        compiler_params=pltpu.CompilerParams(vmem_limit_bytes=40 << 20),
    )(source, order, rows)


def attend_kernel(query_ref, keys_ref, fresh_ref, live_ref, out_ref):
    scale = 1.0 / math.sqrt(HDIM + ROPE)
    across = (((1,), (1,)), ((), ()))
    row = lax.broadcasted_iota(jnp.int32, (TOK, 2 * TOK), 0)
    column = lax.broadcasted_iota(jnp.int32, (TOK, 2 * TOK), 1)
    kept = jnp.where(row + RUN * lax.div(row, RUN) == column, 1.0, 0.0).astype(BF)
    keys = jnp.dot(kept, keys_ref[...], preferred_element_type=F32).astype(BF)
    fresh = fresh_ref[...]
    query = query_ref[...]
    score = lax.dot_general(query, keys, across, preferred_element_type=F32) * scale
    score = jnp.where(live_ref[...] > 0, score, -1e30)
    later = lax.dot_general(query, fresh, across, preferred_element_type=F32) * scale
    row = lax.broadcasted_iota(jnp.int32, later.shape, 0)
    column = lax.broadcasted_iota(jnp.int32, later.shape, 1)
    at_step = lax.rem(lax.div(row, 8), STEPS)
    later = jnp.where(column <= at_step, later, -1e30)
    top = jnp.maximum(jnp.max(score, -1, keepdims=True), jnp.max(later, -1, keepdims=True))
    score = jnp.exp(score - top)
    later = jnp.exp(later - top)
    total = jnp.sum(score, -1, keepdims=True) + jnp.sum(later, -1, keepdims=True)
    inverse = 1.0 / total
    score = (score * inverse).astype(BF)
    later = (later * inverse).astype(BF)
    mixed = jnp.dot(score, keys[:, :LAT], preferred_element_type=F32)
    mixed = mixed + jnp.dot(later, fresh[:, :LAT], preferred_element_type=F32)
    out_ref[...] = mixed.astype(BF)


def attend(query, keys, fresh, live):
    return pl.pallas_call(
        attend_kernel,
        out_shape=jax.ShapeDtypeStruct((query.shape[0], LAT), BF),
        compiler_params=pltpu.CompilerParams(vmem_limit_bytes=24 << 20),
    )(query, keys, fresh, live)


def pick(index, values):
    ids = jnp.arange(values.shape[0], dtype=jnp.int32)
    return jnp.sum(jnp.where(index[..., None] == ids, values, 0), -1)


def groups_of(first):
    found = []
    for core in range(2):
        for x in range(SIDE):
            for other in range(SIDE):
                ring = []
                for k in range(SIDE):
                    y, z = (k, other) if core == first else (other, k)
                    ring.append(((y * SIDE + z) * SIDE + x) * 2 + core)
                found.append(ring)
    return found


def shards(
    hidden, kv_down, kv_gain, uk_weight, uv_weight, queries, new_keys, lengths, assign, block_table
):
    pre_rank = lax.axis_index("pre")
    dec_rank = lax.axis_index("dec")
    both = ("pre", "dec")
    side_y, side_z = pre_rank // SIDE, pre_rank % SIDE
    swapped = side_z * SIDE + side_y
    residue = jnp.where(dec_rank % 2 == 0, pre_rank, swapped)

    counts = (lengths + (REQS - 1)) // REQS
    ends = jnp.cumsum(counts, 1)
    starts = ends - counts
    own_lengths = lax.dynamic_index_in_dim(lengths, dec_rank, 0, keepdims=False)
    own_starts = lax.dynamic_index_in_dim(starts, dec_rank, 0, keepdims=False)
    own_ends = lax.dynamic_index_in_dim(ends, dec_rank, 0, keepdims=False)

    packed = project(lengths, hidden[0].T, kv_down)

    packed = lax.all_to_all(packed, both, 0, 0, tiled=True, axis_index_groups=groups_of(0))
    packed = first_sum(packed)
    packed = lax.all_to_all(packed, both, 0, 0, tiled=True, axis_index_groups=groups_of(1))

    row = jnp.arange(PACK, dtype=jnp.int32)
    inside = (row >= own_starts[:, None]) & (row < own_ends[:, None])
    place = jnp.sum(jnp.where(inside, row - own_starts[:, None], 0), 0)
    limit = jnp.sum(jnp.where(inside, own_lengths[:, None], 0), 0)
    position = place * REQS + residue
    valid = (position < limit).astype(jnp.int32)[None, :]
    half = ROPE // 2
    frequency = 10000.0 ** (-jnp.arange(half, dtype=F32) * 2.0 / ROPE)
    angles = position[None, :].astype(F32) * frequency[:, None]
    rows = finish(packed, kv_gain[:, None], jnp.cos(angles), jnp.sin(angles), valid)

    local_queries = queries[0]
    absorbed = jnp.einsum(
        "bshk,hkl->bshl", local_queries[..., :HDIM], uk_weight, preferred_element_type=F32
    ).astype(BF)
    query_full = jnp.concatenate([absorbed, local_queries[..., HDIM:]], -1)
    query_full = query_full.reshape(REQS, -1, WIDTH)
    rows, query_full = lax.optimization_barrier((rows, query_full))
    everything = lax.all_gather(rows, "dec", axis=1, tiled=True)
    query_full = lax.all_to_all(query_full, "pre", 0, 0, tiled=True)
    everything, query_full = lax.optimization_barrier((everything, query_full))

    slots = lax.dynamic_slice_in_dim(assign, dec_rank * REQS, REQS)
    slot_start = pick(slots, (starts + jnp.arange(starts.shape[0])[:, None] * PACK).reshape(-1))
    slot_count = pick(slots, counts.reshape(-1))
    slot_length = pick(slots, lengths.reshape(-1))
    slot_odd = (slots // REQS) % 2
    run = jnp.arange(RUN, dtype=jnp.int32)
    by_slot = jnp.where(run < slot_count[:, None], slot_start[:, None] + run, -1)
    table = block_table[0]
    pages = table.shape[0]
    page = jnp.arange(pages, dtype=jnp.int32)
    block = jnp.sum(jnp.where(table[None, :] == page[:, None], page[None, :], 0), 1)
    owner, part = block // NPG, block % NPG
    piece = part[:, None] * (RUN // NPG) + jnp.arange(RUN // NPG, dtype=jnp.int32)
    by_page = (owner[:, None] * RUN + piece).reshape(REQS, RUN)
    in_order = jnp.arange(TOK, dtype=jnp.int32).reshape(REQS, RUN)
    order = jnp.concatenate([in_order, by_page], 1).reshape(-1, 1)
    outgoing = select(by_slot.reshape(1, -1), order, everything).reshape(REQS, 2 * RUN, WIDTH)
    arrived = lax.all_to_all(outgoing, "pre", 0, 0, tiled=True)

    sender = jnp.arange(REQS, dtype=jnp.int32)
    sender_swapped = (sender % SIDE) * SIDE + sender // SIDE
    page_odd = pick(owner, slot_odd).reshape(REQS, NPG)
    page_odd = lax.dynamic_index_in_dim(page_odd, pre_rank, 0, keepdims=False)
    sent_residue = jnp.where(page_odd[None, :] == 0, sender[:, None], sender_swapped[:, None])
    target = (
        jnp.arange(NPG, dtype=jnp.int32)[None, :, None] * BLK
        + jnp.arange(RUN // NPG, dtype=jnp.int32)[None, None, :] * REQS
        + sent_residue[:, :, None]
    ).reshape(REQS, RUN)
    target = jnp.concatenate([jnp.full((REQS, RUN), -1, jnp.int32), target], 1).reshape(-1)
    to_place = (jnp.arange(TOK, dtype=jnp.int32)[:, None] == target[None, :]).astype(BF)
    arrived = arrived.reshape(2 * TOK, WIDTH)
    cache = jnp.dot(to_place, arrived, preferred_element_type=F32).astype(BF)

    own_odd = lax.dynamic_index_in_dim(slot_odd, pre_rank, 0, keepdims=False)
    own_length = lax.dynamic_index_in_dim(slot_length, pre_rank, 0, keepdims=False)
    key_residue = jnp.where(own_odd == 0, sender, sender_swapped)
    key_position = run[None, :] * REQS + key_residue[:, None]
    live = (key_position < own_length).astype(jnp.int32).reshape(1, TOK)
    fresh = lax.dynamic_index_in_dim(new_keys[0], pre_rank, 0, keepdims=False)
    fresh = jnp.pad(fresh, ((0, 16 - STEPS), (0, 0)))
    mixed = attend(query_full.reshape(-1, WIDTH), arrived, fresh, live)
    mixed = lax.all_to_all(mixed.reshape(REQS, -1, LAT), "pre", 0, 0, tiled=True)
    mixed = mixed.reshape(REQS, STEPS, -1, LAT)
    attended = jnp.einsum("bshl,hlv->bshv", mixed, uv_weight, preferred_element_type=F32).astype(BF)
    return (cache[None], attended[None])


def solution(mesh):
    return jax.shard_map(
        shards,
        mesh=mesh,
        in_specs=(
            P("dec", None, "pre"),
            P("pre", None),
            P(),
            P("pre", None, None),
            P("pre", None, None),
            P("dec", None, None, "pre", None),
            P("dec", None, None, None),
            P(),
            P(),
            P("dec", None),
        ),
        out_specs=(P("dec", "pre", None), P("dec", None, None, "pre", None)),
        check_vma=False,
    )
```

```python
import functools
import math

import jax
import jax.numpy as jnp
from jax import lax
from jax.experimental import pallas as pl
from jax.experimental.pallas import tpu as pltpu
from jax.sharding import PartitionSpec as P

LAT = 512
ROPE = 64
WIDTH = LAT + ROPE
HDIM = 128
BLK = 64
TOK = 384
REQS = 16
RUN = TOK // REQS
NPG = TOK // BLK
PACK = 256
HOLD = 288
AHEAD = 3
PAIR = 2
SIDE = 4
STEPS = 4

EPS = 1e-06
BF = jnp.bfloat16
F32 = jnp.float32


def project_kernel(
    len_ref, hid_ref, down_ref, out_ref, span_ref, sent_ref, shift_ref, turned_ref, hold_ref, in_sem, out_sem
):
    def load(part):
        where = pl.ds(part * PAIR * TOK, PAIR * TOK)
        return pltpu.make_async_copy(hid_ref.at[:, where], span_ref.at[:, where], in_sem.at[part])

    def store(residue):
        where = residue // SIDE, residue % SIDE
        return pltpu.make_async_copy(sent_ref.at[residue], out_ref.at[where], out_sem.at[residue])

    parts = REQS // PAIR
    for part in range(AHEAD):
        load(part).start()
    hold_ref[...] = jnp.zeros_like(hold_ref)
    turned_ref[...] = down_ref[...].astype(F32).T.astype(BF)
    shape = (REQS, 24, 256)
    offset = lax.broadcasted_iota(jnp.int32, shape, 2)
    offset = offset - lax.broadcasted_iota(jnp.int32, shape, 0)
    shift_ref[...] = offset - REQS * lax.broadcasted_iota(jnp.int32, shape, 1)

    start = 0
    for request in range(REQS):
        part = request // PAIR
        if request % PAIR == 0:
            load(part).wait()
            if part + AHEAD < parts:
                load(part + AHEAD).start()
        length = len_ref[lax.axis_index("dec"), request]
        count = lax.div(length + (REQS - 1), REQS)
        lead = lax.rem(start, 8)
        base = pl.multiple_of(start - lead, 8)

        for first, tokens, window in ((0, 256, 24), (256, 128, 16)):
            begin = request * TOK + first
            hid = span_ref[:, begin : begin + tokens]
            token = lax.broadcasted_iota(jnp.int32, hid.shape, 1)
            hid = jnp.where(token < count * REQS - first, hid, jnp.zeros((), BF))
            chosen = jnp.where(shift_ref[:, :window, :tokens] == -REQS * lead, 1.0, 0.0)
            chosen = chosen.reshape(REQS * window, tokens).astype(BF)
            rows = lax.dot_general(
                chosen, hid, (((1,), (1,)), ((), ())), preferred_element_type=F32
            )
            place = pl.ds(pl.multiple_of(base + first // REQS, 8), window)
            hold_ref[:, place, :] += rows.reshape(REQS, window, -1)

        start = start + count

    for residue in range(REQS):
        rows = hold_ref[residue, :PACK, :].astype(BF)
        sent_ref[residue] = lax.dot_general(
            turned_ref[...], rows, (((1,), (1,)), ((), ())), preferred_element_type=F32
        ).astype(BF)
        store(residue).start()
    for residue in range(REQS):
        store(residue).wait()


def project(lengths, hidden_t, kv_down):
    depth = hidden_t.shape[0]
    return pl.pallas_call(
        project_kernel,
        out_shape=jax.ShapeDtypeStruct((SIDE, SIDE, WIDTH, PACK), BF),
        in_specs=[
            pl.BlockSpec(memory_space=pltpu.SMEM),
            pl.BlockSpec(memory_space=pl.ANY),
            pl.BlockSpec(memory_space=pltpu.VMEM),
        ],
        out_specs=pl.BlockSpec(memory_space=pl.ANY),
        scratch_shapes=[
            pltpu.VMEM((depth, REQS * TOK), BF),
            pltpu.VMEM((REQS, WIDTH, PACK), BF),
            pltpu.VMEM((REQS, 24, 256), jnp.int32),
            pltpu.VMEM((WIDTH, depth), BF),
            pltpu.VMEM((REQS, HOLD, depth), F32),
            pltpu.SemaphoreType.DMA((REQS // PAIR,)),
            pltpu.SemaphoreType.DMA((REQS,)),
        ],
        compiler_params=pltpu.CompilerParams(vmem_limit_bytes=58 << 20),
        cost_estimate=pl.CostEstimate(
            flops=2 * REQS * TOK * depth * WIDTH, bytes_accessed=11 << 20, transcendentals=0
        ),
    )(lengths, hidden_t, kv_down)


def add_up(parts):
    total = parts[0].astype(F32)
    for k in range(1, SIDE):
        total = total + parts[k].astype(F32)
    return total


def first_sum_kernel(parts_ref, out_ref, sent_ref, out_sem):
    def store(part):
        return pltpu.make_async_copy(sent_ref.at[part], out_ref.at[part], out_sem.at[part])

    for part in range(SIDE):
        sent_ref[part] = add_up(parts_ref[:, part]).astype(BF)
        store(part).start()
    for part in range(SIDE):
        store(part).wait()


def first_sum(parts):
    return pl.pallas_call(
        first_sum_kernel,
        out_shape=jax.ShapeDtypeStruct((SIDE, WIDTH, PACK), BF),
        in_specs=[pl.BlockSpec(memory_space=pltpu.VMEM)],
        out_specs=pl.BlockSpec(memory_space=pl.ANY),
        scratch_shapes=[
            pltpu.VMEM((SIDE, WIDTH, PACK), BF),
            pltpu.SemaphoreType.DMA((SIDE,)),
        ],
        compiler_params=pltpu.CompilerParams(vmem_limit_bytes=16 << 20),
    )(parts)


def finish_kernel(parts_ref, gain_ref, cosine_ref, sine_ref, valid_ref, out_ref):
    half = ROPE // 2
    valid = valid_ref[...] > 0
    total = jnp.where(valid, add_up(parts_ref), 0.0)
    latent = total[:LAT]
    scaling = lax.rsqrt(jnp.sum(latent * latent, 0, keepdims=True) / LAT + EPS)
    latent = (latent * scaling * gain_ref[...]).astype(BF)
    first, second = total[LAT : LAT + half], total[LAT + half :]
    cosine, sine = cosine_ref[...], sine_ref[...]
    left = (first * cosine - second * sine).astype(BF)
    right = (second * cosine + first * sine).astype(BF)
    for copy in range(SIDE):
        out_ref[copy, :LAT] = latent
        out_ref[copy, LAT : LAT + half] = left
        out_ref[copy, LAT + half :] = right


def finish(parts, gain, cosine, sine, valid):
    return pl.pallas_call(
        finish_kernel,
        out_shape=jax.ShapeDtypeStruct((SIDE, WIDTH, PACK), BF),
        compiler_params=pltpu.CompilerParams(vmem_limit_bytes=24 << 20),
    )(parts, gain, cosine, sine, valid)


def select_kernel(source_ref, order_ref, near_ref, far_ref, query_ref, out_ref):
    row = lax.broadcasted_iota(jnp.int32, (PACK, TOK), 0)
    mine = jnp.zeros((WIDTH, TOK), F32)
    for side, rows_ref in enumerate((near_ref, far_ref)):
        for x in range(SIDE):
            target = source_ref[side : side + 1, :] - x * PACK
            chosen = jnp.where(row == target, 1.0, 0.0).astype(BF)
            mine = mine + jnp.dot(rows_ref[x], chosen, preferred_element_type=F32)
    column = lax.broadcasted_iota(jnp.int32, (2 * TOK, TOK), 1)
    order = jnp.where(column == order_ref[...], 1.0, 0.0).astype(BF)
    picked = lax.dot_general(
        order, mine.astype(BF), (((1,), (1,)), ((), ())), preferred_element_type=F32
    ).astype(BF)
    out_ref[:, : 2 * RUN] = picked.reshape(REQS, 2 * RUN, WIDTH)
    out_ref[:, 2 * RUN :] = query_ref[...]


def select(source, order, near, far, query):
    return pl.pallas_call(
        select_kernel,
        out_shape=jax.ShapeDtypeStruct((REQS, 2 * RUN + query.shape[1], WIDTH), BF),
        compiler_params=pltpu.CompilerParams(vmem_limit_bytes=40 << 20),
    )(source, order, near, far, query)


def attend_kernel(arrived_ref, fresh_ref, live_ref, out_ref):
    scale = 1.0 / math.sqrt(HDIM + ROPE)
    across = (((1,), (1,)), ((), ()))
    row = lax.broadcasted_iota(jnp.int32, (TOK, 2 * TOK), 0)
    column = lax.broadcasted_iota(jnp.int32, (TOK, 2 * TOK), 1)
    kept = jnp.where(row + RUN * lax.div(row, RUN) == column, 1.0, 0.0).astype(BF)
    rows = arrived_ref[:, : 2 * RUN].reshape(2 * TOK, WIDTH)
    keys = jnp.dot(kept, rows, preferred_element_type=F32).astype(BF)
    fresh = fresh_ref[...]
    query = arrived_ref[:, 2 * RUN :].reshape(-1, WIDTH)
    score = lax.dot_general(query, keys, across, preferred_element_type=F32) * scale
    score = jnp.where(live_ref[...] > 0, score, -1e30)
    later = lax.dot_general(query, fresh, across, preferred_element_type=F32) * scale
    row = lax.broadcasted_iota(jnp.int32, later.shape, 0)
    column = lax.broadcasted_iota(jnp.int32, later.shape, 1)
    at_step = lax.rem(lax.div(row, 8), STEPS)
    later = jnp.where(column <= at_step, later, -1e30)
    top = jnp.maximum(jnp.max(score, -1, keepdims=True), jnp.max(later, -1, keepdims=True))
    score = jnp.exp(score - top)
    later = jnp.exp(later - top)
    total = jnp.sum(score, -1, keepdims=True) + jnp.sum(later, -1, keepdims=True)
    inverse = 1.0 / total
    score = (score * inverse).astype(BF)
    later = (later * inverse).astype(BF)
    mixed = jnp.dot(score, keys[:, :LAT], preferred_element_type=F32)
    mixed = mixed + jnp.dot(later, fresh[:, :LAT], preferred_element_type=F32)
    out_ref[...] = mixed.astype(BF)


def attend(arrived, fresh, live):
    count = REQS * (arrived.shape[1] - 2 * RUN)
    return pl.pallas_call(
        attend_kernel,
        out_shape=jax.ShapeDtypeStruct((count, LAT), BF),
        compiler_params=pltpu.CompilerParams(vmem_limit_bytes=24 << 20),
    )(arrived, fresh, live)


def pick(index, values):
    ids = jnp.arange(values.shape[0], dtype=jnp.int32)
    return jnp.sum(jnp.where(index[..., None] == ids, values, 0), -1)


def groups_of(first):
    found = []
    for core in range(2):
        for x in range(SIDE):
            for other in range(SIDE):
                ring = []
                for k in range(SIDE):
                    y, z = (k, other) if core == first else (other, k)
                    ring.append(((y * SIDE + z) * SIDE + x) * 2 + core)
                found.append(ring)
    return found


def shards(
    hidden, kv_down, kv_gain, uk_weight, uv_weight, queries, new_keys, lengths, assign, block_table
):
    pre_rank = lax.axis_index("pre")
    dec_rank = lax.axis_index("dec")
    both = ("pre", "dec")
    side_y, side_z = pre_rank // SIDE, pre_rank % SIDE
    swapped = side_z * SIDE + side_y
    residue = jnp.where(dec_rank % 2 == 0, pre_rank, swapped)

    counts = (lengths + (REQS - 1)) // REQS
    ends = jnp.cumsum(counts, 1)
    starts = ends - counts
    own_lengths = lax.dynamic_index_in_dim(lengths, dec_rank, 0, keepdims=False)
    own_starts = lax.dynamic_index_in_dim(starts, dec_rank, 0, keepdims=False)
    own_ends = lax.dynamic_index_in_dim(ends, dec_rank, 0, keepdims=False)

    packed = project(lengths, hidden[0].T, kv_down)

    packed = lax.all_to_all(packed, both, 0, 0, tiled=True, axis_index_groups=groups_of(0))
    packed = first_sum(packed)
    packed = lax.all_to_all(packed, both, 0, 0, tiled=True, axis_index_groups=groups_of(1))

    row = jnp.arange(PACK, dtype=jnp.int32)
    inside = (row >= own_starts[:, None]) & (row < own_ends[:, None])
    place = jnp.sum(jnp.where(inside, row - own_starts[:, None], 0), 0)
    limit = jnp.sum(jnp.where(inside, own_lengths[:, None], 0), 0)
    position = place * REQS + residue
    valid = (position < limit).astype(jnp.int32)[None, :]
    half = ROPE // 2
    frequency = 10000.0 ** (-jnp.arange(half, dtype=F32) * 2.0 / ROPE)
    angles = position[None, :].astype(F32) * frequency[:, None]
    rows = finish(packed, kv_gain[:, None], jnp.cos(angles), jnp.sin(angles), valid)

    local_queries = queries[0]
    absorbed = jnp.einsum(
        "bshk,hkl->bshl", local_queries[..., :HDIM], uk_weight, preferred_element_type=F32
    ).astype(BF)
    query_full = jnp.concatenate([absorbed, local_queries[..., HDIM:]], -1)
    query_full = query_full.reshape(REQS, -1, WIDTH)

    along_x = [[2 * x + core for x in range(SIDE)] for core in range(2)]
    near = lax.all_to_all(rows, "dec", 0, 0, tiled=True, axis_index_groups=along_x)
    far = lax.ppermute(near, "dec", [(d, d ^ 1) for d in range(2 * SIDE)])

    slots = lax.dynamic_slice_in_dim(assign, dec_rank * REQS, REQS)
    slot_start = pick(slots, (starts + jnp.arange(starts.shape[0])[:, None] // 2 * PACK).reshape(-1))
    slot_count = pick(slots, counts.reshape(-1))
    slot_length = pick(slots, lengths.reshape(-1))
    slot_odd = (slots // REQS) % 2
    run = jnp.arange(RUN, dtype=jnp.int32)
    by_slot = jnp.where(run < slot_count[:, None], slot_start[:, None] + run, -1)
    is_near = (slot_odd == dec_rank % 2)[:, None]
    source = jnp.stack([jnp.where(is_near, by_slot, -1), jnp.where(is_near, -1, by_slot)])
    table = block_table[0]
    pages = table.shape[0]
    page = jnp.arange(pages, dtype=jnp.int32)
    block = jnp.sum(jnp.where(table[None, :] == page[:, None], page[None, :], 0), 1)
    owner, part = block // NPG, block % NPG
    piece = part[:, None] * (RUN // NPG) + jnp.arange(RUN // NPG, dtype=jnp.int32)
    by_page = (owner[:, None] * RUN + piece).reshape(REQS, RUN)
    in_order = jnp.arange(TOK, dtype=jnp.int32).reshape(REQS, RUN)
    order = jnp.concatenate([in_order, by_page], 1).reshape(-1, 1)
    outgoing = select(source.reshape(2, -1), order, near, far, query_full)
    arrived = lax.all_to_all(outgoing, "pre", 0, 0, tiled=True)

    sender = jnp.arange(REQS, dtype=jnp.int32)
    sender_swapped = (sender % SIDE) * SIDE + sender // SIDE
    page_odd = pick(owner, slot_odd).reshape(REQS, NPG)
    page_odd = lax.dynamic_index_in_dim(page_odd, pre_rank, 0, keepdims=False)
    sent_residue = jnp.where(page_odd[None, :] == 0, sender[:, None], sender_swapped[:, None])
    target = (
        jnp.arange(NPG, dtype=jnp.int32)[None, :, None] * BLK
        + jnp.arange(RUN // NPG, dtype=jnp.int32)[None, None, :] * REQS
        + sent_residue[:, :, None]
    ).reshape(REQS, RUN)
    target = jnp.concatenate([jnp.full((REQS, RUN), -1, jnp.int32), target], 1).reshape(-1)
    to_place = (jnp.arange(TOK, dtype=jnp.int32)[:, None] == target[None, :]).astype(BF)
    placed = arrived[:, : 2 * RUN].reshape(2 * TOK, WIDTH)
    cache = jnp.dot(to_place, placed, preferred_element_type=F32).astype(BF)

    own_odd = lax.dynamic_index_in_dim(slot_odd, pre_rank, 0, keepdims=False)
    own_length = lax.dynamic_index_in_dim(slot_length, pre_rank, 0, keepdims=False)
    key_residue = jnp.where(own_odd == 0, sender, sender_swapped)
    key_position = run[None, :] * REQS + key_residue[:, None]
    live = (key_position < own_length).astype(jnp.int32).reshape(1, TOK)
    fresh = lax.dynamic_index_in_dim(new_keys[0], pre_rank, 0, keepdims=False)
    fresh = jnp.pad(fresh, ((0, 16 - STEPS), (0, 0)))
    mixed = attend(arrived, fresh, live)
    mixed = lax.all_to_all(mixed.reshape(REQS, -1, LAT), "pre", 0, 0, tiled=True)
    mixed = mixed.reshape(REQS, STEPS, -1, LAT)
    attended = jnp.einsum("bshl,hlv->bshv", mixed, uv_weight, preferred_element_type=F32).astype(BF)
    return (cache[None], attended[None])


def solution(mesh):
    return jax.shard_map(
        shards,
        mesh=mesh,
        in_specs=(
            P("dec", None, "pre"),
            P("pre", None),
            P(),
            P("pre", None, None),
            P("pre", None, None),
            P("dec", None, None, "pre", None),
            P("dec", None, None, None),
            P(),
            P(),
            P("dec", None),
        ),
        out_specs=(P("dec", "pre", None), P("dec", None, None, "pre", None)),
        check_vma=False,
    )
```

```python
import functools
import math

import jax
import jax.numpy as jnp
from jax import lax
from jax.experimental import pallas as pl
from jax.experimental.pallas import tpu as pltpu
from jax.sharding import PartitionSpec as P

LAT = 512
ROPE = 64
WIDTH = LAT + ROPE
HDIM = 128
BLK = 64
TOK = 384
REQS = 16
RUN = TOK // REQS
NPG = TOK // BLK
PACK = 256
HOLD = 288
AHEAD = 3
PAIR = 2
SIDE = 4
STEPS = 4

EPS = 1e-06
BF = jnp.bfloat16
F32 = jnp.float32


def halfway(k):
    return (k + SIDE // 2) % SIDE


def turned(rank):
    return halfway(rank // SIDE) * SIDE + halfway(rank % SIDE)


def project_kernel(
    len_ref, hid_ref, down_ref, out_ref, span_ref, sent_ref, shift_ref, turned_ref, hold_ref, in_sem, out_sem
):
    def load(part):
        where = pl.ds(part * PAIR * TOK, PAIR * TOK)
        return pltpu.make_async_copy(hid_ref.at[:, where], span_ref.at[:, where], in_sem.at[part])

    def store(residue):
        where = residue // SIDE, residue % SIDE
        return pltpu.make_async_copy(sent_ref.at[residue], out_ref.at[where], out_sem.at[residue])

    parts = REQS // PAIR
    for part in range(AHEAD):
        load(part).start()
    hold_ref[...] = jnp.zeros_like(hold_ref)
    turned_ref[...] = down_ref[...].astype(F32).T.astype(BF)
    shape = (REQS, 24, 256)
    offset = lax.broadcasted_iota(jnp.int32, shape, 2)
    offset = offset - lax.broadcasted_iota(jnp.int32, shape, 0)
    shift_ref[...] = offset - REQS * lax.broadcasted_iota(jnp.int32, shape, 1)

    start = 0
    for request in range(REQS):
        part = request // PAIR
        if request % PAIR == 0:
            load(part).wait()
            if part + AHEAD < parts:
                load(part + AHEAD).start()
        length = len_ref[lax.axis_index("dec"), request]
        count = lax.div(length + (REQS - 1), REQS)
        lead = lax.rem(start, 8)
        base = pl.multiple_of(start - lead, 8)

        for first, tokens, window in ((0, 256, 24), (256, 128, 16)):
            begin = request * TOK + first
            hid = span_ref[:, begin : begin + tokens]
            token = lax.broadcasted_iota(jnp.int32, hid.shape, 1)
            hid = jnp.where(token < count * REQS - first, hid, jnp.zeros((), BF))
            chosen = jnp.where(shift_ref[:, :window, :tokens] == -REQS * lead, 1.0, 0.0)
            chosen = chosen.reshape(REQS * window, tokens).astype(BF)
            rows = lax.dot_general(
                chosen, hid, (((1,), (1,)), ((), ())), preferred_element_type=F32
            )
            place = pl.ds(pl.multiple_of(base + first // REQS, 8), window)
            hold_ref[:, place, :] += rows.reshape(REQS, window, -1)

        start = start + count

    for residue in range(REQS):
        rows = hold_ref[residue, :PACK, :].astype(BF)
        sent_ref[residue] = lax.dot_general(
            turned_ref[...], rows, (((1,), (1,)), ((), ())), preferred_element_type=F32
        ).astype(BF)
        store(residue).start()
    for residue in range(REQS):
        store(residue).wait()


def project(lengths, hidden_t, kv_down):
    depth = hidden_t.shape[0]
    return pl.pallas_call(
        project_kernel,
        out_shape=jax.ShapeDtypeStruct((SIDE, SIDE, WIDTH, PACK), BF),
        in_specs=[
            pl.BlockSpec(memory_space=pltpu.SMEM),
            pl.BlockSpec(memory_space=pl.ANY),
            pl.BlockSpec(memory_space=pltpu.VMEM),
        ],
        out_specs=pl.BlockSpec(memory_space=pl.ANY),
        scratch_shapes=[
            pltpu.VMEM((depth, REQS * TOK), BF),
            pltpu.VMEM((REQS, WIDTH, PACK), BF),
            pltpu.VMEM((REQS, 24, 256), jnp.int32),
            pltpu.VMEM((WIDTH, depth), BF),
            pltpu.VMEM((REQS, HOLD, depth), F32),
            pltpu.SemaphoreType.DMA((REQS // PAIR,)),
            pltpu.SemaphoreType.DMA((REQS,)),
        ],
        compiler_params=pltpu.CompilerParams(vmem_limit_bytes=58 << 20),
        cost_estimate=pl.CostEstimate(
            flops=2 * REQS * TOK * depth * WIDTH, bytes_accessed=11 << 20, transcendentals=0
        ),
    )(lengths, hidden_t, kv_down)


def add_up(parts):
    total = parts[0].astype(F32)
    for k in range(1, SIDE):
        total = total + parts[k].astype(F32)
    return total


def first_sum_kernel(parts_ref, out_ref, held_ref, sent_ref, in_sem, out_sem):
    def load(part):
        return pltpu.make_async_copy(parts_ref.at[:, part], held_ref.at[part], in_sem.at[part])

    def store(part):
        return pltpu.make_async_copy(sent_ref.at[part], out_ref.at[part], out_sem.at[part])

    for part in range(SIDE):
        load(part).start()
    for part in range(SIDE):
        load(part).wait()
        sent_ref[part] = add_up(held_ref.at[part]).astype(BF)
        store(part).start()
    for part in range(SIDE):
        store(part).wait()


def first_sum(parts):
    whole = pl.BlockSpec(memory_space=pl.ANY)
    return pl.pallas_call(
        first_sum_kernel,
        out_shape=jax.ShapeDtypeStruct((SIDE, WIDTH, PACK), BF),
        in_specs=[whole],
        out_specs=whole,
        scratch_shapes=[
            pltpu.VMEM((SIDE, SIDE, WIDTH, PACK), BF),
            pltpu.VMEM((SIDE, WIDTH, PACK), BF),
            pltpu.SemaphoreType.DMA((SIDE,)),
            pltpu.SemaphoreType.DMA((SIDE,)),
        ],
        compiler_params=pltpu.CompilerParams(vmem_limit_bytes=60 << 20),
    )(parts)


def finish_kernel(parts_ref, gain_ref, cosine_ref, sine_ref, valid_ref, out_ref):
    half = ROPE // 2
    valid = valid_ref[...] > 0
    total = jnp.where(valid, add_up(parts_ref), 0.0)
    latent = total[:LAT]
    scaling = lax.rsqrt(jnp.sum(latent * latent, 0, keepdims=True) / LAT + EPS)
    latent = (latent * scaling * gain_ref[...]).astype(BF)
    first, second = total[LAT : LAT + half], total[LAT + half :]
    cosine, sine = cosine_ref[...], sine_ref[...]
    left = (first * cosine - second * sine).astype(BF)
    right = (second * cosine + first * sine).astype(BF)
    for copy in range(SIDE):
        out_ref[copy, :LAT] = latent
        out_ref[copy, LAT : LAT + half] = left
        out_ref[copy, LAT + half :] = right


def finish(parts, gain, cosine, sine, valid):
    return pl.pallas_call(
        finish_kernel,
        out_shape=jax.ShapeDtypeStruct((SIDE, WIDTH, PACK), BF),
        compiler_params=pltpu.CompilerParams(vmem_limit_bytes=24 << 20),
    )(parts, gain, cosine, sine, valid)


def select_kernel(
    source_ref, order_ref, near_ref, far_ref, query_ref, out_ref, sent_ref, query_sem, out_sem
):
    half = REQS // 2
    held = sent_ref.shape[1]

    def ask(pair):
        begin, source = 2 * pair, turned(2 * pair)
        return pltpu.make_async_copy(
            query_ref.at[pl.ds(source, 2)],
            out_ref.at[pl.ds(begin, 2), pl.ds(held, query_ref.shape[1])],
            query_sem.at[pair],
        )

    for pair in range(half):
        ask(pair).start()
    row = lax.broadcasted_iota(jnp.int32, (PACK, TOK), 0)
    mine = jnp.zeros((WIDTH, TOK), F32)
    for side, rows_ref in enumerate((near_ref, far_ref)):
        for x in range(SIDE):
            target = source_ref[side : side + 1, :] - x * PACK
            chosen = jnp.where(row == target, 1.0, 0.0).astype(BF)
            mine = mine + jnp.dot(rows_ref[x], chosen, preferred_element_type=F32)
    mine = mine.astype(BF)
    column = lax.broadcasted_iota(jnp.int32, (TOK, TOK), 1)

    def store(part):
        where = pl.ds(part * half, half)
        return pltpu.make_async_copy(
            sent_ref.at[where], out_ref.at[where, pl.ds(0, held)], out_sem.at[part]
        )

    for part in range(2):
        order = jnp.where(column == order_ref[part * TOK : (part + 1) * TOK, :], 1.0, 0.0)
        picked = lax.dot_general(
            order.astype(BF), mine, (((1,), (1,)), ((), ())), preferred_element_type=F32
        ).astype(BF)
        sent_ref[part * half : (part + 1) * half] = picked.reshape(half, held, WIDTH)
        store(part).start()
    for pair in range(half):
        ask(pair).wait()
    for part in range(2):
        store(part).wait()


def select(source, order, near, far, query):
    vmem = pl.BlockSpec(memory_space=pltpu.VMEM)
    return pl.pallas_call(
        select_kernel,
        out_shape=jax.ShapeDtypeStruct((REQS, 2 * RUN + query.shape[1], WIDTH), BF),
        in_specs=[vmem] * 5,
        out_specs=pl.BlockSpec(memory_space=pl.ANY),
        scratch_shapes=[
            pltpu.VMEM((REQS, 2 * RUN, WIDTH), BF),
            pltpu.SemaphoreType.DMA((REQS // 2,)),
            pltpu.SemaphoreType.DMA((2,)),
        ],
        compiler_params=pltpu.CompilerParams(vmem_limit_bytes=40 << 20),
    )(source, order, near, far, query)


def attend_kernel(arrived_ref, fresh_ref, live_ref, out_ref):
    scale = 1.0 / math.sqrt(HDIM + ROPE)
    across = (((1,), (1,)), ((), ()))
    row = lax.broadcasted_iota(jnp.int32, (TOK, 2 * TOK), 0)
    column = lax.broadcasted_iota(jnp.int32, (TOK, 2 * TOK), 1)
    kept = jnp.where(row + RUN * lax.div(row, RUN) == column, 1.0, 0.0).astype(BF)
    rows = arrived_ref[:, : 2 * RUN].reshape(2 * TOK, WIDTH)
    keys = jnp.dot(kept, rows, preferred_element_type=F32).astype(BF)
    fresh = fresh_ref[...]
    query = arrived_ref[:, 2 * RUN :].reshape(-1, WIDTH)
    score = lax.dot_general(query, keys, across, preferred_element_type=F32) * scale
    score = jnp.where(live_ref[...] > 0, score, -1e30)
    later = lax.dot_general(query, fresh, across, preferred_element_type=F32) * scale
    row = lax.broadcasted_iota(jnp.int32, later.shape, 0)
    column = lax.broadcasted_iota(jnp.int32, later.shape, 1)
    at_step = lax.rem(lax.div(row, 8), STEPS)
    later = jnp.where(column <= at_step, later, -1e30)
    top = jnp.maximum(jnp.max(score, -1, keepdims=True), jnp.max(later, -1, keepdims=True))
    score = jnp.exp(score - top)
    later = jnp.exp(later - top)
    total = jnp.sum(score, -1, keepdims=True) + jnp.sum(later, -1, keepdims=True)
    inverse = 1.0 / total
    score = (score * inverse).astype(BF)
    later = (later * inverse).astype(BF)
    mixed = jnp.dot(score, keys[:, :LAT], preferred_element_type=F32)
    mixed = mixed + jnp.dot(later, fresh[:, :LAT], preferred_element_type=F32)
    mixed = mixed.astype(BF)
    share = 2 * (arrived_ref.shape[1] - 2 * RUN)
    for pair in range(REQS // 2):
        begin = turned(2 * pair) * share // 2
        out_ref[begin : begin + share] = mixed[pair * share : (pair + 1) * share]


def attend(arrived, fresh, live):
    count = REQS * (arrived.shape[1] - 2 * RUN)
    return pl.pallas_call(
        attend_kernel,
        out_shape=jax.ShapeDtypeStruct((count, LAT), BF),
        compiler_params=pltpu.CompilerParams(vmem_limit_bytes=24 << 20),
    )(arrived, fresh, live)


def pick(index, values):
    ids = jnp.arange(values.shape[0], dtype=jnp.int32)
    return jnp.sum(jnp.where(index[..., None] == ids, values, 0), -1)


def groups_of(first):
    found = []
    for core in range(2):
        for x in range(SIDE):
            for other in range(SIDE):
                ring = []
                for place in range(SIDE):
                    k = halfway(place)
                    y, z = (k, other) if core == first else (other, k)
                    ring.append(((y * SIDE + z) * SIDE + x) * 2 + core)
                found.append(ring)
    return found


def shards(
    hidden, kv_down, kv_gain, uk_weight, uv_weight, queries, new_keys, lengths, assign, block_table
):
    pre_rank = lax.axis_index("pre")
    dec_rank = lax.axis_index("dec")
    both = ("pre", "dec")
    all_pre = [[turned(rank) for rank in range(REQS)]]
    side_y, side_z = halfway(pre_rank // SIDE), halfway(pre_rank % SIDE)
    residue = jnp.where(
        dec_rank % 2 == 0, side_y * SIDE + side_z, side_z * SIDE + side_y
    )

    counts = (lengths + (REQS - 1)) // REQS
    ends = jnp.cumsum(counts, 1)
    starts = ends - counts
    own_lengths = lax.dynamic_index_in_dim(lengths, dec_rank, 0, keepdims=False)
    own_starts = lax.dynamic_index_in_dim(starts, dec_rank, 0, keepdims=False)
    own_ends = lax.dynamic_index_in_dim(ends, dec_rank, 0, keepdims=False)

    packed = project(lengths, hidden[0].T, kv_down)

    packed = lax.all_to_all(packed, both, 0, 0, tiled=True, axis_index_groups=groups_of(0))
    packed = first_sum(packed)
    packed = lax.all_to_all(packed, both, 0, 0, tiled=True, axis_index_groups=groups_of(1))

    row = jnp.arange(PACK, dtype=jnp.int32)
    inside = (row >= own_starts[:, None]) & (row < own_ends[:, None])
    place = jnp.sum(jnp.where(inside, row - own_starts[:, None], 0), 0)
    limit = jnp.sum(jnp.where(inside, own_lengths[:, None], 0), 0)
    position = place * REQS + residue
    valid = (position < limit).astype(jnp.int32)[None, :]
    half = ROPE // 2
    frequency = 10000.0 ** (-jnp.arange(half, dtype=F32) * 2.0 / ROPE)
    angles = position[None, :].astype(F32) * frequency[:, None]
    rows = finish(packed, kv_gain[:, None], jnp.cos(angles), jnp.sin(angles), valid)

    local_queries = queries[0]
    absorbed = jnp.einsum(
        "bshk,hkl->bshl", local_queries[..., :HDIM], uk_weight, preferred_element_type=F32
    ).astype(BF)
    query_full = jnp.concatenate([absorbed, local_queries[..., HDIM:]], -1)
    query_full = query_full.reshape(REQS, -1, WIDTH)

    along_x = [[2 * halfway(x) + core for x in range(SIDE)] for core in range(2)]
    near = lax.all_to_all(rows, "dec", 0, 0, tiled=True, axis_index_groups=along_x)
    far = lax.ppermute(near, "dec", [(d, d ^ 1) for d in range(2 * SIDE)])

    slots = lax.dynamic_slice_in_dim(assign, dec_rank * REQS, REQS)
    column = halfway(jnp.arange(starts.shape[0], dtype=jnp.int32)[:, None] // 2)
    slot_start = pick(slots, (starts + column * PACK).reshape(-1))
    slot_count = pick(slots, counts.reshape(-1))
    slot_length = pick(slots, lengths.reshape(-1))
    slot_odd = (slots // REQS) % 2
    run = jnp.arange(RUN, dtype=jnp.int32)
    by_slot = jnp.where(run < slot_count[:, None], slot_start[:, None] + run, -1)
    is_near = (slot_odd == dec_rank % 2)[:, None]
    source = jnp.stack([jnp.where(is_near, by_slot, -1), jnp.where(is_near, -1, by_slot)])
    table = block_table[0]
    pages = table.shape[0]
    page = jnp.arange(pages, dtype=jnp.int32)
    block = jnp.sum(jnp.where(table[None, :] == page[:, None], page[None, :], 0), 1)
    owner, part = block // NPG, block % NPG
    piece = part[:, None] * (RUN // NPG) + jnp.arange(RUN // NPG, dtype=jnp.int32)
    by_page = (owner[:, None] * RUN + piece).reshape(REQS, RUN)
    in_order = jnp.arange(TOK, dtype=jnp.int32).reshape(REQS, RUN)
    order = jnp.concatenate([in_order, by_page], 1)
    order = order.reshape(SIDE, SIDE, -1)
    order = jnp.roll(order, (SIDE // 2, SIDE // 2), (0, 1)).reshape(-1, 1)
    outgoing = select(source.reshape(2, -1), order, near, far, query_full)
    arrived = lax.all_to_all(outgoing, "pre", 0, 0, tiled=True, axis_index_groups=all_pre)

    sender = jnp.arange(REQS, dtype=jnp.int32)
    sender_swapped = (sender % SIDE) * SIDE + sender // SIDE
    page_odd = pick(owner, slot_odd).reshape(REQS, NPG)
    page_odd = lax.dynamic_index_in_dim(page_odd, pre_rank, 0, keepdims=False)
    sent_residue = jnp.where(page_odd[None, :] == 0, sender[:, None], sender_swapped[:, None])
    target = (
        jnp.arange(NPG, dtype=jnp.int32)[None, :, None] * BLK
        + jnp.arange(RUN // NPG, dtype=jnp.int32)[None, None, :] * REQS
        + sent_residue[:, :, None]
    ).reshape(REQS, RUN)
    target = jnp.concatenate([jnp.full((REQS, RUN), -1, jnp.int32), target], 1).reshape(-1)
    to_place = (jnp.arange(TOK, dtype=jnp.int32)[:, None] == target[None, :]).astype(BF)
    placed = arrived[:, : 2 * RUN].reshape(2 * TOK, WIDTH)
    cache = jnp.dot(to_place, placed, preferred_element_type=F32).astype(BF)

    own_odd = lax.dynamic_index_in_dim(slot_odd, pre_rank, 0, keepdims=False)
    own_length = lax.dynamic_index_in_dim(slot_length, pre_rank, 0, keepdims=False)
    key_residue = jnp.where(own_odd == 0, sender, sender_swapped)
    key_position = run[None, :] * REQS + key_residue[:, None]
    live = (key_position < own_length).astype(jnp.int32).reshape(1, TOK)
    fresh = lax.dynamic_index_in_dim(new_keys[0], pre_rank, 0, keepdims=False)
    fresh = jnp.pad(fresh, ((0, 16 - STEPS), (0, 0)))
    mixed = attend(arrived, fresh, live)
    mixed = mixed.reshape(REQS, -1, LAT)
    mixed = lax.all_to_all(mixed, "pre", 0, 0, tiled=True)
    mixed = mixed.reshape(REQS, STEPS, -1, LAT)
    attended = jnp.einsum("bshl,hlv->bshv", mixed, uv_weight, preferred_element_type=F32).astype(BF)
    return (cache[None], attended[None])


def solution(mesh):
    return jax.shard_map(
        shards,
        mesh=mesh,
        in_specs=(
            P("dec", None, "pre"),
            P("pre", None),
            P(),
            P("pre", None, None),
            P("pre", None, None),
            P("dec", None, None, "pre", None),
            P("dec", None, None, None),
            P(),
            P(),
            P("dec", None),
        ),
        out_specs=(P("dec", "pre", None), P("dec", None, None, "pre", None)),
        check_vma=False,
    )
```

```python
import functools
import math

import jax
import jax.numpy as jnp
from jax import lax
from jax.experimental import pallas as pl
from jax.experimental.pallas import tpu as pltpu
from jax.sharding import PartitionSpec as P

LAT = 512
ROPE = 64
WIDTH = LAT + ROPE
HDIM = 128
BLK = 64
TOK = 384
REQS = 16
RUN = TOK // REQS
NPG = TOK // BLK
PACK = 256
HOLD = 288
AHEAD = 3
PAIR = 2
SIDE = 4
HALF = 2
STEPS = 4

EPS = 1e-06
BF = jnp.bfloat16
F32 = jnp.float32


def project_kernel(
    len_ref, hid_ref, down_w_ref, up_ref, down_ref, wait_ref, own_ref,
    span_ref, shift_ref, turned_ref, hold_ref, wait_hold_ref, own_hold_ref, in_sem, out_sem,
):
    def load(part):
        where = pl.ds(part * PAIR * TOK, PAIR * TOK)
        return pltpu.make_async_copy(hid_ref.at[:, where], span_ref.at[:, where], in_sem.at[part])

    keep_own = pltpu.make_async_copy(own_hold_ref, own_ref, out_sem.at[0])
    keep_wait = pltpu.make_async_copy(wait_hold_ref, wait_ref, out_sem.at[1])

    parts = REQS // PAIR
    for part in range(AHEAD):
        load(part).start()
    hold_ref[...] = jnp.zeros_like(hold_ref)
    turned_ref[...] = down_w_ref[...].astype(F32).T.astype(BF)
    shape = (REQS, 24, 256)
    offset = lax.broadcasted_iota(jnp.int32, shape, 2)
    offset = offset - lax.broadcasted_iota(jnp.int32, shape, 0)
    shift_ref[...] = offset - REQS * lax.broadcasted_iota(jnp.int32, shape, 1)

    start = 0
    for request in range(REQS):
        part = request // PAIR
        if request % PAIR == 0:
            load(part).wait()
            if part + AHEAD < parts:
                load(part + AHEAD).start()
        length = len_ref[lax.axis_index("dec"), request]
        count = lax.div(length + (REQS - 1), REQS)
        lead = lax.rem(start, 8)
        base = pl.multiple_of(start - lead, 8)

        for first, tokens, window in ((0, 256, 24), (256, 128, 16)):
            begin = request * TOK + first
            hid = span_ref[:, begin : begin + tokens]
            token = lax.broadcasted_iota(jnp.int32, hid.shape, 1)
            hid = jnp.where(token < count * REQS - first, hid, jnp.zeros((), BF))
            chosen = jnp.where(shift_ref[:, :window, :tokens] == -REQS * lead, 1.0, 0.0)
            chosen = chosen.reshape(REQS * window, tokens).astype(BF)
            rows = lax.dot_general(
                chosen, hid, (((1,), (1,)), ((), ())), preferred_element_type=F32
            )
            place = pl.ds(pl.multiple_of(base + first // REQS, 8), window)
            hold_ref[:, place, :] += rows.reshape(REQS, window, -1)

        start = start + count

    pre_rank, dec_rank = lax.axis_index("pre"), lax.axis_index("dec")
    place = jnp.where(
        lax.rem(dec_rank, 2) == 0, lax.div(pre_rank, SIDE), lax.rem(pre_rank, SIDE)
    )
    for away in (0, 1, 3, 2):
        for item in range(SIDE):
            residue = lax.rem(place + away, SIDE) * SIDE + item
            rows = hold_ref[residue, :PACK, :].astype(BF)
            part = lax.dot_general(
                turned_ref[...], rows, (((1,), (1,)), ((), ())), preferred_element_type=F32
            )
            late, lane = item // HALF, item % HALF
            if away == 0:
                own_hold_ref[item] = part
            elif away == 1 and late:
                up_ref[1, lane] = part.astype(BF)
            elif away == 1:
                wait_hold_ref[0, lane] = part
            elif away == 3 and late:
                wait_hold_ref[1, lane] = part
            elif away == 3:
                down_ref[1, lane] = part.astype(BF)
            elif late:
                down_ref[0, lane] = part.astype(BF)
            else:
                up_ref[0, lane] = part.astype(BF)
        if away == 0:
            keep_own.start()
        elif away == 3:
            keep_wait.start()
    keep_own.wait()
    keep_wait.wait()


def project(lengths, hidden_t, kv_down):
    depth = hidden_t.shape[0]
    vmem = pl.BlockSpec(memory_space=pltpu.VMEM)
    pair = (2, HALF, WIDTH, PACK)
    return pl.pallas_call(
        project_kernel,
        out_shape=(
            jax.ShapeDtypeStruct(pair, BF),
            jax.ShapeDtypeStruct(pair, BF),
            jax.ShapeDtypeStruct(pair, F32),
            jax.ShapeDtypeStruct((SIDE, WIDTH, PACK), F32),
        ),
        in_specs=[
            pl.BlockSpec(memory_space=pltpu.SMEM),
            pl.BlockSpec(memory_space=pl.ANY),
            vmem,
        ],
        out_specs=(vmem, vmem, pl.BlockSpec(memory_space=pl.ANY), pl.BlockSpec(memory_space=pl.ANY)),
        scratch_shapes=[
            pltpu.VMEM((depth, REQS * TOK), BF),
            pltpu.VMEM((REQS, 24, 256), jnp.int32),
            pltpu.VMEM((WIDTH, depth), BF),
            pltpu.VMEM((REQS, HOLD, depth), F32),
            pltpu.VMEM(pair, F32),
            pltpu.VMEM((SIDE, WIDTH, PACK), F32),
            pltpu.SemaphoreType.DMA((REQS // PAIR,)),
            pltpu.SemaphoreType.DMA((2,)),
        ],
        compiler_params=pltpu.CompilerParams(vmem_limit_bytes=50 << 20),
        cost_estimate=pl.CostEstimate(
            flops=2 * REQS * TOK * depth * WIDTH, bytes_accessed=11 << 20, transcendentals=0
        ),
    )(lengths, hidden_t, kv_down)


def relay_kernel(wait_ref, from_below_ref, from_above_ref, up_ref, down_ref):
    up_ref[...] = (wait_ref[0] + from_below_ref[0].astype(F32)).astype(BF)
    down_ref[...] = (wait_ref[1] + from_above_ref[0].astype(F32)).astype(BF)


def relay(wait, from_below, from_above):
    shape = jax.ShapeDtypeStruct((HALF, WIDTH, PACK), BF)
    return pl.pallas_call(
        relay_kernel,
        out_shape=(shape, shape),
        compiler_params=pltpu.CompilerParams(vmem_limit_bytes=8 << 20),
    )(wait, from_below, from_above)


def add_up(parts):
    total = parts[0].astype(F32)
    for k in range(1, SIDE):
        total = total + parts[k].astype(F32)
    return total


def first_sum_kernel(own_ref, below_ref, above_ref, late_below_ref, late_above_ref, out_ref):
    for item in range(HALF):
        out_ref[item] = (
            own_ref[item] + late_below_ref[item].astype(F32) + above_ref[1, item].astype(F32)
        ).astype(BF)
        out_ref[HALF + item] = (
            own_ref[HALF + item] + below_ref[1, item].astype(F32) + late_above_ref[item].astype(F32)
        ).astype(BF)


def first_sum(own, below, above, late_below, late_above):
    return pl.pallas_call(
        first_sum_kernel,
        out_shape=jax.ShapeDtypeStruct((SIDE, WIDTH, PACK), BF),
        compiler_params=pltpu.CompilerParams(vmem_limit_bytes=8 << 20),
    )(own, below, above, late_below, late_above)


def finish_kernel(parts_ref, gain_ref, cosine_ref, sine_ref, valid_ref, out_ref):
    half = ROPE // 2
    valid = valid_ref[...] > 0
    total = jnp.where(valid, add_up(parts_ref), 0.0)
    latent = total[:LAT]
    scaling = lax.rsqrt(jnp.sum(latent * latent, 0, keepdims=True) / LAT + EPS)
    latent = (latent * scaling * gain_ref[...]).astype(BF)
    first, second = total[LAT : LAT + half], total[LAT + half :]
    cosine, sine = cosine_ref[...], sine_ref[...]
    left = (first * cosine - second * sine).astype(BF)
    right = (second * cosine + first * sine).astype(BF)
    for copy in range(SIDE):
        out_ref[copy, :LAT] = latent
        out_ref[copy, LAT : LAT + half] = left
        out_ref[copy, LAT + half :] = right


def finish(parts, gain, cosine, sine, valid):
    return pl.pallas_call(
        finish_kernel,
        out_shape=jax.ShapeDtypeStruct((SIDE, WIDTH, PACK), BF),
        compiler_params=pltpu.CompilerParams(vmem_limit_bytes=24 << 20),
    )(parts, gain, cosine, sine, valid)


def select_kernel(source_ref, order_ref, near_ref, far_ref, query_ref, out_ref):
    row = lax.broadcasted_iota(jnp.int32, (PACK, TOK), 0)
    mine = jnp.zeros((WIDTH, TOK), F32)
    for side, rows_ref in enumerate((near_ref, far_ref)):
        for x in range(SIDE):
            target = source_ref[side : side + 1, :] - x * PACK
            chosen = jnp.where(row == target, 1.0, 0.0).astype(BF)
            mine = mine + jnp.dot(rows_ref[x], chosen, preferred_element_type=F32)
    column = lax.broadcasted_iota(jnp.int32, (2 * TOK, TOK), 1)
    order = jnp.where(column == order_ref[...], 1.0, 0.0).astype(BF)
    picked = lax.dot_general(
        order, mine.astype(BF), (((1,), (1,)), ((), ())), preferred_element_type=F32
    ).astype(BF)
    out_ref[:, : 2 * RUN] = picked.reshape(REQS, 2 * RUN, WIDTH)
    out_ref[:, 2 * RUN :] = query_ref[...]


def select(source, order, near, far, query):
    return pl.pallas_call(
        select_kernel,
        out_shape=jax.ShapeDtypeStruct((REQS, 2 * RUN + query.shape[1], WIDTH), BF),
        compiler_params=pltpu.CompilerParams(vmem_limit_bytes=40 << 20),
    )(source, order, near, far, query)


def attend_kernel(arrived_ref, fresh_ref, live_ref, out_ref):
    scale = 1.0 / math.sqrt(HDIM + ROPE)
    across = (((1,), (1,)), ((), ()))
    row = lax.broadcasted_iota(jnp.int32, (TOK, 2 * TOK), 0)
    column = lax.broadcasted_iota(jnp.int32, (TOK, 2 * TOK), 1)
    kept = jnp.where(row + RUN * lax.div(row, RUN) == column, 1.0, 0.0).astype(BF)
    rows = arrived_ref[:, : 2 * RUN].reshape(2 * TOK, WIDTH)
    keys = jnp.dot(kept, rows, preferred_element_type=F32).astype(BF)
    fresh = fresh_ref[...]
    query = arrived_ref[:, 2 * RUN :].reshape(-1, WIDTH)
    score = lax.dot_general(query, keys, across, preferred_element_type=F32) * scale
    score = jnp.where(live_ref[...] > 0, score, -1e30)
    later = lax.dot_general(query, fresh, across, preferred_element_type=F32) * scale
    row = lax.broadcasted_iota(jnp.int32, later.shape, 0)
    column = lax.broadcasted_iota(jnp.int32, later.shape, 1)
    at_step = lax.rem(lax.div(row, 8), STEPS)
    later = jnp.where(column <= at_step, later, -1e30)
    top = jnp.maximum(jnp.max(score, -1, keepdims=True), jnp.max(later, -1, keepdims=True))
    score = jnp.exp(score - top)
    later = jnp.exp(later - top)
    total = jnp.sum(score, -1, keepdims=True) + jnp.sum(later, -1, keepdims=True)
    inverse = 1.0 / total
    score = (score * inverse).astype(BF)
    later = (later * inverse).astype(BF)
    mixed = jnp.dot(score, keys[:, :LAT], preferred_element_type=F32)
    mixed = mixed + jnp.dot(later, fresh[:, :LAT], preferred_element_type=F32)
    out_ref[...] = mixed.astype(BF)


def attend(arrived, fresh, live):
    count = REQS * (arrived.shape[1] - 2 * RUN)
    return pl.pallas_call(
        attend_kernel,
        out_shape=jax.ShapeDtypeStruct((count, LAT), BF),
        compiler_params=pltpu.CompilerParams(vmem_limit_bytes=24 << 20),
    )(arrived, fresh, live)


def pick(index, values):
    ids = jnp.arange(values.shape[0], dtype=jnp.int32)
    return jnp.sum(jnp.where(index[..., None] == ids, values, 0), -1)


def groups_of(first):
    found = []
    for core in range(2):
        for x in range(SIDE):
            for other in range(SIDE):
                ring = []
                for k in range(SIDE):
                    y, z = (k, other) if core == first else (other, k)
                    ring.append(((y * SIDE + z) * SIDE + x) * 2 + core)
                found.append(ring)
    return found


def neighbours(step):
    pairs = []
    for pre in range(REQS):
        y, z = pre // SIDE, pre % SIDE
        for dec in range(2 * SIDE):
            ny, nz = ((y + step) % SIDE, z) if dec % 2 == 0 else (y, (z + step) % SIDE)
            pairs.append((pre * 2 * SIDE + dec, (ny * SIDE + nz) * 2 * SIDE + dec))
    return pairs


def shards(
    hidden, kv_down, kv_gain, uk_weight, uv_weight, queries, new_keys, lengths, assign, block_table
):
    pre_rank = lax.axis_index("pre")
    dec_rank = lax.axis_index("dec")
    both = ("pre", "dec")
    side_y, side_z = pre_rank // SIDE, pre_rank % SIDE
    swapped = side_z * SIDE + side_y
    residue = jnp.where(dec_rank % 2 == 0, pre_rank, swapped)

    counts = (lengths + (REQS - 1)) // REQS
    ends = jnp.cumsum(counts, 1)
    starts = ends - counts
    own_lengths = lax.dynamic_index_in_dim(lengths, dec_rank, 0, keepdims=False)
    own_starts = lax.dynamic_index_in_dim(starts, dec_rank, 0, keepdims=False)
    own_ends = lax.dynamic_index_in_dim(ends, dec_rank, 0, keepdims=False)

    up, down, wait, own = project(lengths, hidden[0].T, kv_down)

    below = lax.ppermute(up, both, neighbours(1))
    above = lax.ppermute(down, both, neighbours(-1))
    up, down = relay(wait, below, above)
    late_below = lax.ppermute(up, both, neighbours(1))
    late_above = lax.ppermute(down, both, neighbours(-1))
    packed = first_sum(own, below, above, late_below, late_above)
    packed = lax.all_to_all(packed, both, 0, 0, tiled=True, axis_index_groups=groups_of(1))

    row = jnp.arange(PACK, dtype=jnp.int32)
    inside = (row >= own_starts[:, None]) & (row < own_ends[:, None])
    place = jnp.sum(jnp.where(inside, row - own_starts[:, None], 0), 0)
    limit = jnp.sum(jnp.where(inside, own_lengths[:, None], 0), 0)
    position = place * REQS + residue
    valid = (position < limit).astype(jnp.int32)[None, :]
    half = ROPE // 2
    frequency = 10000.0 ** (-jnp.arange(half, dtype=F32) * 2.0 / ROPE)
    angles = position[None, :].astype(F32) * frequency[:, None]
    rows = finish(packed, kv_gain[:, None], jnp.cos(angles), jnp.sin(angles), valid)

    local_queries = queries[0]
    absorbed = jnp.einsum(
        "bshk,hkl->bshl", local_queries[..., :HDIM], uk_weight, preferred_element_type=F32
    ).astype(BF)
    query_full = jnp.concatenate([absorbed, local_queries[..., HDIM:]], -1)
    query_full = query_full.reshape(REQS, -1, WIDTH)

    along_x = [[2 * x + core for x in range(SIDE)] for core in range(2)]
    near = lax.all_to_all(rows, "dec", 0, 0, tiled=True, axis_index_groups=along_x)
    far = lax.ppermute(near, "dec", [(d, d ^ 1) for d in range(2 * SIDE)])

    slots = lax.dynamic_slice_in_dim(assign, dec_rank * REQS, REQS)
    slot_start = pick(slots, (starts + jnp.arange(starts.shape[0])[:, None] // 2 * PACK).reshape(-1))
    slot_count = pick(slots, counts.reshape(-1))
    slot_length = pick(slots, lengths.reshape(-1))
    slot_odd = (slots // REQS) % 2
    run = jnp.arange(RUN, dtype=jnp.int32)
    by_slot = jnp.where(run < slot_count[:, None], slot_start[:, None] + run, -1)
    is_near = (slot_odd == dec_rank % 2)[:, None]
    source = jnp.stack([jnp.where(is_near, by_slot, -1), jnp.where(is_near, -1, by_slot)])
    table = block_table[0]
    pages = table.shape[0]
    page = jnp.arange(pages, dtype=jnp.int32)
    block = jnp.sum(jnp.where(table[None, :] == page[:, None], page[None, :], 0), 1)
    owner, part = block // NPG, block % NPG
    piece = part[:, None] * (RUN // NPG) + jnp.arange(RUN // NPG, dtype=jnp.int32)
    by_page = (owner[:, None] * RUN + piece).reshape(REQS, RUN)
    in_order = jnp.arange(TOK, dtype=jnp.int32).reshape(REQS, RUN)
    order = jnp.concatenate([in_order, by_page], 1).reshape(-1, 1)
    outgoing = select(source.reshape(2, -1), order, near, far, query_full)
    arrived = lax.all_to_all(outgoing, "pre", 0, 0, tiled=True)

    sender = jnp.arange(REQS, dtype=jnp.int32)
    sender_swapped = (sender % SIDE) * SIDE + sender // SIDE
    page_odd = pick(owner, slot_odd).reshape(REQS, NPG)
    page_odd = lax.dynamic_index_in_dim(page_odd, pre_rank, 0, keepdims=False)
    sent_residue = jnp.where(page_odd[None, :] == 0, sender[:, None], sender_swapped[:, None])
    target = (
        jnp.arange(NPG, dtype=jnp.int32)[None, :, None] * BLK
        + jnp.arange(RUN // NPG, dtype=jnp.int32)[None, None, :] * REQS
        + sent_residue[:, :, None]
    ).reshape(REQS, RUN)
    target = jnp.concatenate([jnp.full((REQS, RUN), -1, jnp.int32), target], 1).reshape(-1)
    to_place = (jnp.arange(TOK, dtype=jnp.int32)[:, None] == target[None, :]).astype(BF)
    placed = arrived[:, : 2 * RUN].reshape(2 * TOK, WIDTH)
    cache = jnp.dot(to_place, placed, preferred_element_type=F32).astype(BF)

    own_odd = lax.dynamic_index_in_dim(slot_odd, pre_rank, 0, keepdims=False)
    own_length = lax.dynamic_index_in_dim(slot_length, pre_rank, 0, keepdims=False)
    key_residue = jnp.where(own_odd == 0, sender, sender_swapped)
    key_position = run[None, :] * REQS + key_residue[:, None]
    live = (key_position < own_length).astype(jnp.int32).reshape(1, TOK)
    fresh = lax.dynamic_index_in_dim(new_keys[0], pre_rank, 0, keepdims=False)
    fresh = jnp.pad(fresh, ((0, 16 - STEPS), (0, 0)))
    mixed = attend(arrived, fresh, live)
    mixed = lax.all_to_all(mixed.reshape(REQS, -1, LAT), "pre", 0, 0, tiled=True)
    mixed = mixed.reshape(REQS, STEPS, -1, LAT)
    attended = jnp.einsum("bshl,hlv->bshv", mixed, uv_weight, preferred_element_type=F32).astype(BF)
    return (cache[None], attended[None])


def solution(mesh):
    return jax.shard_map(
        shards,
        mesh=mesh,
        in_specs=(
            P("dec", None, "pre"),
            P("pre", None),
            P(),
            P("pre", None, None),
            P("pre", None, None),
            P("dec", None, None, "pre", None),
            P("dec", None, None, None),
            P(),
            P(),
            P("dec", None),
        ),
        out_specs=(P("dec", "pre", None), P("dec", None, None, "pre", None)),
        check_vma=False,
    )
```

```python
import functools
import math

import jax
import jax.numpy as jnp
from jax import lax
from jax.experimental import pallas as pl
from jax.experimental.pallas import tpu as pltpu
from jax.sharding import PartitionSpec as P

LAT = 512
ROPE = 64
WIDTH = LAT + ROPE
HDIM = 128
BLK = 64
TOK = 384
REQS = 16
RUN = TOK // REQS
NPG = TOK // BLK
PACK = 256
HOLD = 288
AHEAD = 3
PAIR = 2
SIDE = 4
HALF = 2
STEPS = 4

EPS = 1e-06
BF = jnp.bfloat16
F32 = jnp.float32


def project_kernel(
    len_ref, hid_ref, down_w_ref, up_ref, down_ref, wait_ref, own_ref,
    span_ref, shift_ref, turned_ref, hold_ref, wait_hold_ref, own_hold_ref, in_sem, out_sem,
):
    def load(part):
        where = pl.ds(part * PAIR * TOK, PAIR * TOK)
        return pltpu.make_async_copy(hid_ref.at[:, where], span_ref.at[:, where], in_sem.at[part])

    keep_own = pltpu.make_async_copy(own_hold_ref, own_ref, out_sem.at[0])
    keep_wait = pltpu.make_async_copy(wait_hold_ref, wait_ref, out_sem.at[1])

    parts = REQS // PAIR
    for part in range(AHEAD):
        load(part).start()
    hold_ref[...] = jnp.zeros_like(hold_ref)
    turned_ref[...] = down_w_ref[...].astype(F32).T.astype(BF)
    shape = (REQS, 24, 256)
    offset = lax.broadcasted_iota(jnp.int32, shape, 2)
    offset = offset - lax.broadcasted_iota(jnp.int32, shape, 0)
    shift_ref[...] = offset - REQS * lax.broadcasted_iota(jnp.int32, shape, 1)

    start = 0
    for request in range(REQS):
        part = request // PAIR
        if request % PAIR == 0:
            load(part).wait()
            if part + AHEAD < parts:
                load(part + AHEAD).start()
        length = len_ref[lax.axis_index("dec"), request]
        count = lax.div(length + (REQS - 1), REQS)
        lead = lax.rem(start, 8)
        base = pl.multiple_of(start - lead, 8)

        for first, tokens, window in ((0, 256, 24), (256, 128, 16)):
            begin = request * TOK + first
            hid = span_ref[:, begin : begin + tokens]
            token = lax.broadcasted_iota(jnp.int32, hid.shape, 1)
            hid = jnp.where(token < count * REQS - first, hid, jnp.zeros((), BF))
            chosen = jnp.where(shift_ref[:, :window, :tokens] == -REQS * lead, 1.0, 0.0)
            chosen = chosen.reshape(REQS * window, tokens).astype(BF)
            rows = lax.dot_general(
                chosen, hid, (((1,), (1,)), ((), ())), preferred_element_type=F32
            )
            place = pl.ds(pl.multiple_of(base + first // REQS, 8), window)
            hold_ref[:, place, :] += rows.reshape(REQS, window, -1)

        start = start + count

    pre_rank, dec_rank = lax.axis_index("pre"), lax.axis_index("dec")
    place = jnp.where(
        lax.rem(dec_rank, 2) == 0, lax.div(pre_rank, SIDE), lax.rem(pre_rank, SIDE)
    )
    for away in (0, 1, 3, 2):
        for item in range(SIDE):
            residue = lax.rem(place + away, SIDE) * SIDE + item
            rows = hold_ref[residue, :PACK, :].astype(BF)
            part = lax.dot_general(
                turned_ref[...], rows, (((1,), (1,)), ((), ())), preferred_element_type=F32
            )
            late, lane = item // HALF, item % HALF
            if away == 0:
                own_hold_ref[item] = part
            elif away == 1 and late:
                up_ref[1, lane] = part.astype(BF)
            elif away == 1:
                wait_hold_ref[0, lane] = part
            elif away == 3 and late:
                wait_hold_ref[1, lane] = part
            elif away == 3:
                down_ref[1, lane] = part.astype(BF)
            elif late:
                down_ref[0, lane] = part.astype(BF)
            else:
                up_ref[0, lane] = part.astype(BF)
        if away == 0:
            keep_own.start()
        elif away == 3:
            keep_wait.start()
    keep_own.wait()
    keep_wait.wait()


def project(lengths, hidden_t, kv_down):
    depth = hidden_t.shape[0]
    vmem = pl.BlockSpec(memory_space=pltpu.VMEM)
    pair = (2, HALF, WIDTH, PACK)
    return pl.pallas_call(
        project_kernel,
        out_shape=(
            jax.ShapeDtypeStruct(pair, BF),
            jax.ShapeDtypeStruct(pair, BF),
            jax.ShapeDtypeStruct(pair, F32),
            jax.ShapeDtypeStruct((SIDE, WIDTH, PACK), F32),
        ),
        in_specs=[
            pl.BlockSpec(memory_space=pltpu.SMEM),
            pl.BlockSpec(memory_space=pl.ANY),
            vmem,
        ],
        out_specs=(vmem, vmem, pl.BlockSpec(memory_space=pl.ANY), pl.BlockSpec(memory_space=pl.ANY)),
        scratch_shapes=[
            pltpu.VMEM((depth, REQS * TOK), BF),
            pltpu.VMEM((REQS, 24, 256), jnp.int32),
            pltpu.VMEM((WIDTH, depth), BF),
            pltpu.VMEM((REQS, HOLD, depth), F32),
            pltpu.VMEM(pair, F32),
            pltpu.VMEM((SIDE, WIDTH, PACK), F32),
            pltpu.SemaphoreType.DMA((REQS // PAIR,)),
            pltpu.SemaphoreType.DMA((2,)),
        ],
        compiler_params=pltpu.CompilerParams(vmem_limit_bytes=50 << 20),
        cost_estimate=pl.CostEstimate(
            flops=2 * REQS * TOK * depth * WIDTH, bytes_accessed=11 << 20, transcendentals=0
        ),
    )(lengths, hidden_t, kv_down)


def stage_kernel(share_ref, out_ref, sem):
    copy = pltpu.make_async_copy(share_ref, out_ref, sem)
    copy.start()
    copy.wait()


def stage(share):
    return pl.pallas_call(
        stage_kernel,
        out_shape=jax.ShapeDtypeStruct(share.shape, F32),
        in_specs=[pl.BlockSpec(memory_space=pl.ANY)],
        out_specs=pl.BlockSpec(memory_space=pltpu.VMEM),
        scratch_shapes=[pltpu.SemaphoreType.DMA],
        compiler_params=pltpu.CompilerParams(vmem_limit_bytes=8 << 20),
        cost_estimate=pl.CostEstimate(flops=0, bytes_accessed=5 << 20, transcendentals=0),
    )(share)


def relay_kernel(wait_ref, from_below_ref, from_above_ref, up_ref, down_ref):
    up_ref[...] = (wait_ref[0] + from_below_ref[0].astype(F32)).astype(BF)
    down_ref[...] = (wait_ref[1] + from_above_ref[0].astype(F32)).astype(BF)


def relay(wait, from_below, from_above):
    shape = jax.ShapeDtypeStruct((HALF, WIDTH, PACK), BF)
    return pl.pallas_call(
        relay_kernel,
        out_shape=(shape, shape),
        compiler_params=pltpu.CompilerParams(vmem_limit_bytes=8 << 20),
    )(wait, from_below, from_above)


def add_up(parts):
    total = parts[0].astype(F32)
    for k in range(1, SIDE):
        total = total + parts[k].astype(F32)
    return total


def first_sum_kernel(own_ref, below_ref, above_ref, late_below_ref, late_above_ref, out_ref):
    for item in range(HALF):
        out_ref[item] = (
            own_ref[item] + late_below_ref[item].astype(F32) + above_ref[1, item].astype(F32)
        ).astype(BF)
        out_ref[HALF + item] = (
            own_ref[HALF + item] + below_ref[1, item].astype(F32) + late_above_ref[item].astype(F32)
        ).astype(BF)


def first_sum(own, below, above, late_below, late_above):
    return pl.pallas_call(
        first_sum_kernel,
        out_shape=jax.ShapeDtypeStruct((SIDE, WIDTH, PACK), BF),
        compiler_params=pltpu.CompilerParams(vmem_limit_bytes=8 << 20),
    )(own, below, above, late_below, late_above)


def finish_kernel(parts_ref, gain_ref, cosine_ref, sine_ref, valid_ref, out_ref):
    half = ROPE // 2
    valid = valid_ref[...] > 0
    total = jnp.where(valid, add_up(parts_ref), 0.0)
    latent = total[:LAT]
    scaling = lax.rsqrt(jnp.sum(latent * latent, 0, keepdims=True) / LAT + EPS)
    latent = (latent * scaling * gain_ref[...]).astype(BF)
    first, second = total[LAT : LAT + half], total[LAT + half :]
    cosine, sine = cosine_ref[...], sine_ref[...]
    left = (first * cosine - second * sine).astype(BF)
    right = (second * cosine + first * sine).astype(BF)
    for copy in range(SIDE):
        out_ref[copy, :LAT] = latent
        out_ref[copy, LAT : LAT + half] = left
        out_ref[copy, LAT + half :] = right


def finish(parts, gain, cosine, sine, valid):
    return pl.pallas_call(
        finish_kernel,
        out_shape=jax.ShapeDtypeStruct((SIDE, WIDTH, PACK), BF),
        compiler_params=pltpu.CompilerParams(vmem_limit_bytes=24 << 20),
    )(parts, gain, cosine, sine, valid)


def select_kernel(source_ref, order_ref, near_ref, far_ref, query_ref, out_ref):
    row = lax.broadcasted_iota(jnp.int32, (PACK, TOK), 0)
    mine = jnp.zeros((WIDTH, TOK), F32)
    for side, rows_ref in enumerate((near_ref, far_ref)):
        for x in range(SIDE):
            target = source_ref[side : side + 1, :] - x * PACK
            chosen = jnp.where(row == target, 1.0, 0.0).astype(BF)
            mine = mine + jnp.dot(rows_ref[x], chosen, preferred_element_type=F32)
    column = lax.broadcasted_iota(jnp.int32, (2 * TOK, TOK), 1)
    order = jnp.where(column == order_ref[...], 1.0, 0.0).astype(BF)
    picked = lax.dot_general(
        order, mine.astype(BF), (((1,), (1,)), ((), ())), preferred_element_type=F32
    ).astype(BF)
    out_ref[:, : 2 * RUN] = picked.reshape(REQS, 2 * RUN, WIDTH)
    out_ref[:, 2 * RUN :] = query_ref[...]


def select(source, order, near, far, query):
    return pl.pallas_call(
        select_kernel,
        out_shape=jax.ShapeDtypeStruct((REQS, 2 * RUN + query.shape[1], WIDTH), BF),
        compiler_params=pltpu.CompilerParams(vmem_limit_bytes=40 << 20),
    )(source, order, near, far, query)


def attend_kernel(arrived_ref, fresh_ref, live_ref, out_ref):
    scale = 1.0 / math.sqrt(HDIM + ROPE)
    across = (((1,), (1,)), ((), ()))
    row = lax.broadcasted_iota(jnp.int32, (TOK, 2 * TOK), 0)
    column = lax.broadcasted_iota(jnp.int32, (TOK, 2 * TOK), 1)
    kept = jnp.where(row + RUN * lax.div(row, RUN) == column, 1.0, 0.0).astype(BF)
    rows = arrived_ref[:, : 2 * RUN].reshape(2 * TOK, WIDTH)
    keys = jnp.dot(kept, rows, preferred_element_type=F32).astype(BF)
    fresh = fresh_ref[...]
    query = arrived_ref[:, 2 * RUN :].reshape(-1, WIDTH)
    score = lax.dot_general(query, keys, across, preferred_element_type=F32) * scale
    score = jnp.where(live_ref[...] > 0, score, -1e30)
    later = lax.dot_general(query, fresh, across, preferred_element_type=F32) * scale
    row = lax.broadcasted_iota(jnp.int32, later.shape, 0)
    column = lax.broadcasted_iota(jnp.int32, later.shape, 1)
    at_step = lax.rem(lax.div(row, 8), STEPS)
    later = jnp.where(column <= at_step, later, -1e30)
    top = jnp.maximum(jnp.max(score, -1, keepdims=True), jnp.max(later, -1, keepdims=True))
    score = jnp.exp(score - top)
    later = jnp.exp(later - top)
    total = jnp.sum(score, -1, keepdims=True) + jnp.sum(later, -1, keepdims=True)
    inverse = 1.0 / total
    score = (score * inverse).astype(BF)
    later = (later * inverse).astype(BF)
    mixed = jnp.dot(score, keys[:, :LAT], preferred_element_type=F32)
    mixed = mixed + jnp.dot(later, fresh[:, :LAT], preferred_element_type=F32)
    out_ref[...] = mixed.astype(BF)


def attend(arrived, fresh, live):
    count = REQS * (arrived.shape[1] - 2 * RUN)
    return pl.pallas_call(
        attend_kernel,
        out_shape=jax.ShapeDtypeStruct((count, LAT), BF),
        compiler_params=pltpu.CompilerParams(vmem_limit_bytes=24 << 20),
    )(arrived, fresh, live)


def pick(index, values):
    ids = jnp.arange(values.shape[0], dtype=jnp.int32)
    return jnp.sum(jnp.where(index[..., None] == ids, values, 0), -1)


def groups_of(first):
    found = []
    for core in range(2):
        for x in range(SIDE):
            for other in range(SIDE):
                ring = []
                for k in range(SIDE):
                    y, z = (k, other) if core == first else (other, k)
                    ring.append(((y * SIDE + z) * SIDE + x) * 2 + core)
                found.append(ring)
    return found


def neighbours(step):
    pairs = []
    for pre in range(REQS):
        y, z = pre // SIDE, pre % SIDE
        for dec in range(2 * SIDE):
            ny, nz = ((y + step) % SIDE, z) if dec % 2 == 0 else (y, (z + step) % SIDE)
            pairs.append((pre * 2 * SIDE + dec, (ny * SIDE + nz) * 2 * SIDE + dec))
    return pairs


def shards(
    hidden, kv_down, kv_gain, uk_weight, uv_weight, queries, new_keys, lengths, assign, block_table
):
    pre_rank = lax.axis_index("pre")
    dec_rank = lax.axis_index("dec")
    both = ("pre", "dec")
    side_y, side_z = pre_rank // SIDE, pre_rank % SIDE
    swapped = side_z * SIDE + side_y
    residue = jnp.where(dec_rank % 2 == 0, pre_rank, swapped)

    counts = (lengths + (REQS - 1)) // REQS
    ends = jnp.cumsum(counts, 1)
    starts = ends - counts
    own_lengths = lax.dynamic_index_in_dim(lengths, dec_rank, 0, keepdims=False)
    own_starts = lax.dynamic_index_in_dim(starts, dec_rank, 0, keepdims=False)
    own_ends = lax.dynamic_index_in_dim(ends, dec_rank, 0, keepdims=False)

    up, down, wait, own = project(lengths, hidden[0].T, kv_down)

    below = lax.ppermute(up, both, neighbours(1))
    above = lax.ppermute(down, both, neighbours(-1))
    up, down = relay(stage(wait), below, above)
    own, up, down = lax.optimization_barrier((own, up, down))
    late_below = lax.ppermute(up, both, neighbours(1))
    late_above = lax.ppermute(down, both, neighbours(-1))
    packed = first_sum(stage(own), below, above, late_below, late_above)
    packed = lax.all_to_all(packed, both, 0, 0, tiled=True, axis_index_groups=groups_of(1))

    row = jnp.arange(PACK, dtype=jnp.int32)
    inside = (row >= own_starts[:, None]) & (row < own_ends[:, None])
    place = jnp.sum(jnp.where(inside, row - own_starts[:, None], 0), 0)
    limit = jnp.sum(jnp.where(inside, own_lengths[:, None], 0), 0)
    position = place * REQS + residue
    valid = (position < limit).astype(jnp.int32)[None, :]
    half = ROPE // 2
    frequency = 10000.0 ** (-jnp.arange(half, dtype=F32) * 2.0 / ROPE)
    angles = position[None, :].astype(F32) * frequency[:, None]
    rows = finish(packed, kv_gain[:, None], jnp.cos(angles), jnp.sin(angles), valid)

    local_queries = queries[0]
    absorbed = jnp.einsum(
        "bshk,hkl->bshl", local_queries[..., :HDIM], uk_weight, preferred_element_type=F32
    ).astype(BF)
    query_full = jnp.concatenate([absorbed, local_queries[..., HDIM:]], -1)
    query_full = query_full.reshape(REQS, -1, WIDTH)

    along_x = [[2 * x + core for x in range(SIDE)] for core in range(2)]
    near = lax.all_to_all(rows, "dec", 0, 0, tiled=True, axis_index_groups=along_x)
    far = lax.ppermute(near, "dec", [(d, d ^ 1) for d in range(2 * SIDE)])

    slots = lax.dynamic_slice_in_dim(assign, dec_rank * REQS, REQS)
    slot_start = pick(slots, (starts + jnp.arange(starts.shape[0])[:, None] // 2 * PACK).reshape(-1))
    slot_count = pick(slots, counts.reshape(-1))
    slot_length = pick(slots, lengths.reshape(-1))
    slot_odd = (slots // REQS) % 2
    run = jnp.arange(RUN, dtype=jnp.int32)
    by_slot = jnp.where(run < slot_count[:, None], slot_start[:, None] + run, -1)
    is_near = (slot_odd == dec_rank % 2)[:, None]
    source = jnp.stack([jnp.where(is_near, by_slot, -1), jnp.where(is_near, -1, by_slot)])
    table = block_table[0]
    pages = table.shape[0]
    page = jnp.arange(pages, dtype=jnp.int32)
    block = jnp.sum(jnp.where(table[None, :] == page[:, None], page[None, :], 0), 1)
    owner, part = block // NPG, block % NPG
    piece = part[:, None] * (RUN // NPG) + jnp.arange(RUN // NPG, dtype=jnp.int32)
    by_page = (owner[:, None] * RUN + piece).reshape(REQS, RUN)
    in_order = jnp.arange(TOK, dtype=jnp.int32).reshape(REQS, RUN)
    order = jnp.concatenate([in_order, by_page], 1).reshape(-1, 1)
    outgoing = select(source.reshape(2, -1), order, near, far, query_full)
    arrived = lax.all_to_all(outgoing, "pre", 0, 0, tiled=True)

    sender = jnp.arange(REQS, dtype=jnp.int32)
    sender_swapped = (sender % SIDE) * SIDE + sender // SIDE
    page_odd = pick(owner, slot_odd).reshape(REQS, NPG)
    page_odd = lax.dynamic_index_in_dim(page_odd, pre_rank, 0, keepdims=False)
    sent_residue = jnp.where(page_odd[None, :] == 0, sender[:, None], sender_swapped[:, None])
    target = (
        jnp.arange(NPG, dtype=jnp.int32)[None, :, None] * BLK
        + jnp.arange(RUN // NPG, dtype=jnp.int32)[None, None, :] * REQS
        + sent_residue[:, :, None]
    ).reshape(REQS, RUN)
    target = jnp.concatenate([jnp.full((REQS, RUN), -1, jnp.int32), target], 1).reshape(-1)
    to_place = (jnp.arange(TOK, dtype=jnp.int32)[:, None] == target[None, :]).astype(BF)
    placed = arrived[:, : 2 * RUN].reshape(2 * TOK, WIDTH)
    cache = jnp.dot(to_place, placed, preferred_element_type=F32).astype(BF)

    own_odd = lax.dynamic_index_in_dim(slot_odd, pre_rank, 0, keepdims=False)
    own_length = lax.dynamic_index_in_dim(slot_length, pre_rank, 0, keepdims=False)
    key_residue = jnp.where(own_odd == 0, sender, sender_swapped)
    key_position = run[None, :] * REQS + key_residue[:, None]
    live = (key_position < own_length).astype(jnp.int32).reshape(1, TOK)
    fresh = lax.dynamic_index_in_dim(new_keys[0], pre_rank, 0, keepdims=False)
    fresh = jnp.pad(fresh, ((0, 16 - STEPS), (0, 0)))
    mixed = attend(arrived, fresh, live)
    mixed = lax.all_to_all(mixed.reshape(REQS, -1, LAT), "pre", 0, 0, tiled=True)
    mixed = mixed.reshape(REQS, STEPS, -1, LAT)
    attended = jnp.einsum("bshl,hlv->bshv", mixed, uv_weight, preferred_element_type=F32).astype(BF)
    return (cache[None], attended[None])


def solution(mesh):
    return jax.shard_map(
        shards,
        mesh=mesh,
        in_specs=(
            P("dec", None, "pre"),
            P("pre", None),
            P(),
            P("pre", None, None),
            P("pre", None, None),
            P("dec", None, None, "pre", None),
            P("dec", None, None, None),
            P(),
            P(),
            P("dec", None),
        ),
        out_specs=(P("dec", "pre", None), P("dec", None, None, "pre", None)),
        check_vma=False,
    )
```

```python
import functools
import math

import jax
import jax.numpy as jnp
from jax import lax
from jax.experimental import pallas as pl
from jax.experimental.pallas import tpu as pltpu
from jax.sharding import PartitionSpec as P

LAT = 512
ROPE = 64
WIDTH = LAT + ROPE
HDIM = 128
BLK = 64
TOK = 384
REQS = 16
RUN = TOK // REQS
NPG = TOK // BLK
PACK = 256
HOLD = 288
AHEAD = 3
PAIR = 2
SIDE = 4
HALF = 2
STEPS = 4

EPS = 1e-06
BF = jnp.bfloat16
F32 = jnp.float32


def project_kernel(
    len_ref, hid_ref, down_w_ref, up_ref, down_ref, wait_ref, own_ref,
    span_ref, shift_ref, turned_ref, hold_ref, wait_hold_ref, own_hold_ref, in_sem, out_sem,
):
    def load(part):
        where = pl.ds(part * PAIR * TOK, PAIR * TOK)
        return pltpu.make_async_copy(hid_ref.at[:, where], span_ref.at[:, where], in_sem.at[part])

    keep_own = pltpu.make_async_copy(own_hold_ref, own_ref, out_sem.at[0])
    keep_wait = pltpu.make_async_copy(wait_hold_ref, wait_ref, out_sem.at[1])

    parts = REQS // PAIR
    for part in range(AHEAD):
        load(part).start()
    hold_ref[...] = jnp.zeros_like(hold_ref)
    turned_ref[...] = down_w_ref[...].astype(F32).T.astype(BF)
    shape = (REQS, 24, 256)
    offset = lax.broadcasted_iota(jnp.int32, shape, 2)
    offset = offset - lax.broadcasted_iota(jnp.int32, shape, 0)
    shift_ref[...] = offset - REQS * lax.broadcasted_iota(jnp.int32, shape, 1)

    start = 0
    for request in range(REQS):
        part = request // PAIR
        if request % PAIR == 0:
            load(part).wait()
            if part + AHEAD < parts:
                load(part + AHEAD).start()
        length = len_ref[lax.axis_index("dec"), request]
        count = lax.div(length + (REQS - 1), REQS)
        lead = lax.rem(start, 8)
        base = pl.multiple_of(start - lead, 8)

        for first, tokens, window in ((0, 256, 24), (256, 128, 16)):
            begin = request * TOK + first
            hid = span_ref[:, begin : begin + tokens]
            token = lax.broadcasted_iota(jnp.int32, hid.shape, 1)
            hid = jnp.where(token < count * REQS - first, hid, jnp.zeros((), BF))
            chosen = jnp.where(shift_ref[:, :window, :tokens] == -REQS * lead, 1.0, 0.0)
            chosen = chosen.reshape(REQS * window, tokens).astype(BF)
            rows = lax.dot_general(
                chosen, hid, (((1,), (1,)), ((), ())), preferred_element_type=F32
            )
            place = pl.ds(pl.multiple_of(base + first // REQS, 8), window)
            hold_ref[:, place, :] += rows.reshape(REQS, window, -1)

        start = start + count

    pre_rank, dec_rank = lax.axis_index("pre"), lax.axis_index("dec")
    along_y, along_z = lax.div(pre_rank, SIDE), lax.rem(pre_rank, SIDE)
    even = lax.rem(dec_rank, 2) == 0
    place, other = jnp.where(even, along_y, along_z), jnp.where(even, along_z, along_y)
    for away in (0, 1, 3, 2):
        for item in range(SIDE):
            residue = lax.rem(place + away, SIDE) * SIDE + lax.rem(other + item, SIDE)
            rows = hold_ref[residue, :PACK, :].astype(BF)
            part = lax.dot_general(
                turned_ref[...], rows, (((1,), (1,)), ((), ())), preferred_element_type=F32
            )
            late, lane = item // HALF, item % HALF
            if away == 0:
                own_hold_ref[item] = part
            elif away == 1 and late:
                up_ref[1, lane] = part.astype(BF)
            elif away == 1:
                wait_hold_ref[0, lane] = part
            elif away == 3 and late:
                wait_hold_ref[1, lane] = part
            elif away == 3:
                down_ref[1, lane] = part.astype(BF)
            elif late:
                down_ref[0, lane] = part.astype(BF)
            else:
                up_ref[0, lane] = part.astype(BF)
        if away == 0:
            keep_own.start()
        elif away == 3:
            keep_wait.start()
    keep_own.wait()
    keep_wait.wait()


def project(lengths, hidden_t, kv_down):
    depth = hidden_t.shape[0]
    vmem = pl.BlockSpec(memory_space=pltpu.VMEM)
    pair = (2, HALF, WIDTH, PACK)
    return pl.pallas_call(
        project_kernel,
        out_shape=(
            jax.ShapeDtypeStruct(pair, BF),
            jax.ShapeDtypeStruct(pair, BF),
            jax.ShapeDtypeStruct(pair, F32),
            jax.ShapeDtypeStruct((SIDE, WIDTH, PACK), F32),
        ),
        in_specs=[
            pl.BlockSpec(memory_space=pltpu.SMEM),
            pl.BlockSpec(memory_space=pl.ANY),
            vmem,
        ],
        out_specs=(vmem, vmem, pl.BlockSpec(memory_space=pl.ANY), pl.BlockSpec(memory_space=pl.ANY)),
        scratch_shapes=[
            pltpu.VMEM((depth, REQS * TOK), BF),
            pltpu.VMEM((REQS, 24, 256), jnp.int32),
            pltpu.VMEM((WIDTH, depth), BF),
            pltpu.VMEM((REQS, HOLD, depth), F32),
            pltpu.VMEM(pair, F32),
            pltpu.VMEM((SIDE, WIDTH, PACK), F32),
            pltpu.SemaphoreType.DMA((REQS // PAIR,)),
            pltpu.SemaphoreType.DMA((2,)),
        ],
        compiler_params=pltpu.CompilerParams(vmem_limit_bytes=58 << 20),
        cost_estimate=pl.CostEstimate(
            flops=2 * REQS * TOK * depth * WIDTH, bytes_accessed=11 << 20, transcendentals=0
        ),
    )(lengths, hidden_t, kv_down)


def stage_kernel(share_ref, out_ref, sem):
    copy = pltpu.make_async_copy(share_ref, out_ref, sem)
    copy.start()
    copy.wait()


def stage(share):
    return pl.pallas_call(
        stage_kernel,
        out_shape=jax.ShapeDtypeStruct(share.shape, F32),
        in_specs=[pl.BlockSpec(memory_space=pl.ANY)],
        out_specs=pl.BlockSpec(memory_space=pltpu.VMEM),
        scratch_shapes=[pltpu.SemaphoreType.DMA],
        compiler_params=pltpu.CompilerParams(vmem_limit_bytes=8 << 20),
        cost_estimate=pl.CostEstimate(flops=0, bytes_accessed=5 << 20, transcendentals=0),
    )(share)


def relay_kernel(wait_ref, from_below_ref, from_above_ref, up_ref, down_ref):
    up_ref[...] = (wait_ref[0] + from_below_ref[0].astype(F32)).astype(BF)
    down_ref[...] = (wait_ref[1] + from_above_ref[0].astype(F32)).astype(BF)


def relay(wait, from_below, from_above):
    shape = jax.ShapeDtypeStruct((HALF, WIDTH, PACK), BF)
    return pl.pallas_call(
        relay_kernel,
        out_shape=(shape, shape),
        compiler_params=pltpu.CompilerParams(vmem_limit_bytes=8 << 20),
    )(wait, from_below, from_above)


def first_sum_kernel(
    own_ref, below_ref, above_ref, late_below_ref, late_above_ref, kept_ref, *out_refs
):
    for item in range(SIDE):
        lane = item % HALF
        if item < HALF:
            more = late_below_ref[lane].astype(F32) + above_ref[1, lane].astype(F32)
        else:
            more = below_ref[1, lane].astype(F32) + late_above_ref[lane].astype(F32)
        total = own_ref[item] + more
        if item == 0:
            kept_ref[...] = total
        else:
            out_refs[item - 1][...] = total.astype(BF)


def first_sum(own, below, above, late_below, late_above):
    share = (WIDTH, PACK)
    return pl.pallas_call(
        first_sum_kernel,
        out_shape=(jax.ShapeDtypeStruct(share, F32),)
        + (jax.ShapeDtypeStruct(share, BF),) * (SIDE - 1),
        compiler_params=pltpu.CompilerParams(vmem_limit_bytes=8 << 20),
    )(own, below, above, late_below, late_above)


def finish_kernel(
    kept_ref, one_ref, two_ref, three_ref, gain_ref, cosine_ref, sine_ref, valid_ref, out_ref):
    half = ROPE // 2
    valid = valid_ref[...] > 0
    total = kept_ref[...]
    for share_ref in (one_ref, two_ref, three_ref):
        total = total + share_ref[...].astype(F32)
    total = jnp.where(valid, total, 0.0)
    latent = total[:LAT]
    scaling = lax.rsqrt(jnp.sum(latent * latent, 0, keepdims=True) / LAT + EPS)
    latent = (latent * scaling * gain_ref[...]).astype(BF)
    first, second = total[LAT : LAT + half], total[LAT + half :]
    cosine, sine = cosine_ref[...], sine_ref[...]
    left = (first * cosine - second * sine).astype(BF)
    right = (second * cosine + first * sine).astype(BF)
    for copy in range(SIDE):
        out_ref[copy, :LAT] = latent
        out_ref[copy, LAT : LAT + half] = left
        out_ref[copy, LAT + half :] = right


def finish(kept, one, two, three, gain, cosine, sine, valid):
    return pl.pallas_call(
        finish_kernel,
        out_shape=jax.ShapeDtypeStruct((SIDE, WIDTH, PACK), BF),
        compiler_params=pltpu.CompilerParams(vmem_limit_bytes=24 << 20),
    )(kept, one, two, three, gain, cosine, sine, valid)


def select_kernel(source_ref, order_ref, near_ref, far_ref, query_ref, out_ref):
    row = lax.broadcasted_iota(jnp.int32, (PACK, TOK), 0)
    mine = jnp.zeros((WIDTH, TOK), F32)
    for side, rows_ref in enumerate((near_ref, far_ref)):
        for x in range(SIDE):
            target = source_ref[side : side + 1, :] - x * PACK
            chosen = jnp.where(row == target, 1.0, 0.0).astype(BF)
            mine = mine + jnp.dot(rows_ref[x], chosen, preferred_element_type=F32)
    column = lax.broadcasted_iota(jnp.int32, (2 * TOK, TOK), 1)
    order = jnp.where(column == order_ref[...], 1.0, 0.0).astype(BF)
    picked = lax.dot_general(
        order, mine.astype(BF), (((1,), (1,)), ((), ())), preferred_element_type=F32
    ).astype(BF)
    out_ref[:, : 2 * RUN] = picked.reshape(REQS, 2 * RUN, WIDTH)
    out_ref[:, 2 * RUN :] = query_ref[...]


def select(source, order, near, far, query):
    return pl.pallas_call(
        select_kernel,
        out_shape=jax.ShapeDtypeStruct((REQS, 2 * RUN + query.shape[1], WIDTH), BF),
        compiler_params=pltpu.CompilerParams(vmem_limit_bytes=40 << 20),
    )(source, order, near, far, query)


def attend_kernel(arrived_ref, fresh_ref, live_ref, out_ref):
    scale = 1.0 / math.sqrt(HDIM + ROPE)
    across = (((1,), (1,)), ((), ()))
    row = lax.broadcasted_iota(jnp.int32, (TOK, 2 * TOK), 0)
    column = lax.broadcasted_iota(jnp.int32, (TOK, 2 * TOK), 1)
    kept = jnp.where(row + RUN * lax.div(row, RUN) == column, 1.0, 0.0).astype(BF)
    rows = arrived_ref[:, : 2 * RUN].reshape(2 * TOK, WIDTH)
    keys = jnp.dot(kept, rows, preferred_element_type=F32).astype(BF)
    fresh = fresh_ref[...]
    query = arrived_ref[:, 2 * RUN :].reshape(-1, WIDTH)
    score = lax.dot_general(query, keys, across, preferred_element_type=F32) * scale
    score = jnp.where(live_ref[...] > 0, score, -1e30)
    later = lax.dot_general(query, fresh, across, preferred_element_type=F32) * scale
    row = lax.broadcasted_iota(jnp.int32, later.shape, 0)
    column = lax.broadcasted_iota(jnp.int32, later.shape, 1)
    at_step = lax.rem(lax.div(row, 8), STEPS)
    later = jnp.where(column <= at_step, later, -1e30)
    top = jnp.maximum(jnp.max(score, -1, keepdims=True), jnp.max(later, -1, keepdims=True))
    score = jnp.exp(score - top)
    later = jnp.exp(later - top)
    total = jnp.sum(score, -1, keepdims=True) + jnp.sum(later, -1, keepdims=True)
    inverse = 1.0 / total
    score = (score * inverse).astype(BF)
    later = (later * inverse).astype(BF)
    mixed = jnp.dot(score, keys[:, :LAT], preferred_element_type=F32)
    mixed = mixed + jnp.dot(later, fresh[:, :LAT], preferred_element_type=F32)
    out_ref[...] = mixed.astype(BF)


def attend(arrived, fresh, live):
    count = REQS * (arrived.shape[1] - 2 * RUN)
    return pl.pallas_call(
        attend_kernel,
        out_shape=jax.ShapeDtypeStruct((count, LAT), BF),
        compiler_params=pltpu.CompilerParams(vmem_limit_bytes=24 << 20),
    )(arrived, fresh, live)


def pick(index, values):
    ids = jnp.arange(values.shape[0], dtype=jnp.int32)
    return jnp.sum(jnp.where(index[..., None] == ids, values, 0), -1)


def neighbours(step, turn=0):
    pairs = []
    for pre in range(REQS):
        y, z = pre // SIDE, pre % SIDE
        for dec in range(2 * SIDE):
            up_y = dec % 2 == turn
            ny, nz = ((y + step) % SIDE, z) if up_y else (y, (z + step) % SIDE)
            pairs.append((pre * 2 * SIDE + dec, (ny * SIDE + nz) * 2 * SIDE + dec))
    return pairs


def shards(
    hidden, kv_down, kv_gain, uk_weight, uv_weight, queries, new_keys, lengths, assign, block_table
):
    pre_rank = lax.axis_index("pre")
    dec_rank = lax.axis_index("dec")
    both = ("pre", "dec")
    side_y, side_z = pre_rank // SIDE, pre_rank % SIDE
    swapped = side_z * SIDE + side_y
    residue = jnp.where(dec_rank % 2 == 0, pre_rank, swapped)

    counts = (lengths + (REQS - 1)) // REQS
    ends = jnp.cumsum(counts, 1)
    starts = ends - counts
    own_lengths = lax.dynamic_index_in_dim(lengths, dec_rank, 0, keepdims=False)
    own_starts = lax.dynamic_index_in_dim(starts, dec_rank, 0, keepdims=False)
    own_ends = lax.dynamic_index_in_dim(ends, dec_rank, 0, keepdims=False)

    up, down, wait, own = project(lengths, hidden[0].T, kv_down)

    below = lax.ppermute(up, both, neighbours(1))
    above = lax.ppermute(down, both, neighbours(-1))
    up, down = relay(stage(wait), below, above)
    own, up, down = lax.optimization_barrier((own, up, down))
    late_below = lax.ppermute(up, both, neighbours(1))
    late_above = lax.ppermute(down, both, neighbours(-1))
    kept, *shares = first_sum(stage(own), below, above, late_below, late_above)
    shares = [lax.ppermute(part, both, neighbours(k + 1, 1)) for k, part in enumerate(shares)]

    row = jnp.arange(PACK, dtype=jnp.int32)
    inside = (row >= own_starts[:, None]) & (row < own_ends[:, None])
    place = jnp.sum(jnp.where(inside, row - own_starts[:, None], 0), 0)
    limit = jnp.sum(jnp.where(inside, own_lengths[:, None], 0), 0)
    position = place * REQS + residue
    valid = (position < limit).astype(jnp.int32)[None, :]
    half = ROPE // 2
    frequency = 10000.0 ** (-jnp.arange(half, dtype=F32) * 2.0 / ROPE)
    angles = position[None, :].astype(F32) * frequency[:, None]
    rows = finish(kept, *shares, kv_gain[:, None], jnp.cos(angles), jnp.sin(angles), valid)

    local_queries = queries[0]
    absorbed = jnp.einsum(
        "bshk,hkl->bshl", local_queries[..., :HDIM], uk_weight, preferred_element_type=F32
    ).astype(BF)
    query_full = jnp.concatenate([absorbed, local_queries[..., HDIM:]], -1)
    query_full = query_full.reshape(REQS, -1, WIDTH)

    along_x = [[2 * x + core for x in range(SIDE)] for core in range(2)]
    near = lax.all_to_all(rows, "dec", 0, 0, tiled=True, axis_index_groups=along_x)
    far = lax.ppermute(near, "dec", [(d, d ^ 1) for d in range(2 * SIDE)])

    slots = lax.dynamic_slice_in_dim(assign, dec_rank * REQS, REQS)
    slot_start = pick(slots, (starts + jnp.arange(starts.shape[0])[:, None] // 2 * PACK).reshape(-1))
    slot_count = pick(slots, counts.reshape(-1))
    slot_length = pick(slots, lengths.reshape(-1))
    slot_odd = (slots // REQS) % 2
    run = jnp.arange(RUN, dtype=jnp.int32)
    by_slot = jnp.where(run < slot_count[:, None], slot_start[:, None] + run, -1)
    is_near = (slot_odd == dec_rank % 2)[:, None]
    source = jnp.stack([jnp.where(is_near, by_slot, -1), jnp.where(is_near, -1, by_slot)])
    table = block_table[0]
    pages = table.shape[0]
    page = jnp.arange(pages, dtype=jnp.int32)
    block = jnp.sum(jnp.where(table[None, :] == page[:, None], page[None, :], 0), 1)
    owner, part = block // NPG, block % NPG
    piece = part[:, None] * (RUN // NPG) + jnp.arange(RUN // NPG, dtype=jnp.int32)
    by_page = (owner[:, None] * RUN + piece).reshape(REQS, RUN)
    in_order = jnp.arange(TOK, dtype=jnp.int32).reshape(REQS, RUN)
    order = jnp.concatenate([in_order, by_page], 1).reshape(-1, 1)
    outgoing = select(source.reshape(2, -1), order, near, far, query_full)
    arrived = lax.all_to_all(outgoing, "pre", 0, 0, tiled=True)

    sender = jnp.arange(REQS, dtype=jnp.int32)
    sender_swapped = (sender % SIDE) * SIDE + sender // SIDE
    page_odd = pick(owner, slot_odd).reshape(REQS, NPG)
    page_odd = lax.dynamic_index_in_dim(page_odd, pre_rank, 0, keepdims=False)
    sent_residue = jnp.where(page_odd[None, :] == 0, sender[:, None], sender_swapped[:, None])
    target = (
        jnp.arange(NPG, dtype=jnp.int32)[None, :, None] * BLK
        + jnp.arange(RUN // NPG, dtype=jnp.int32)[None, None, :] * REQS
        + sent_residue[:, :, None]
    ).reshape(REQS, RUN)
    target = jnp.concatenate([jnp.full((REQS, RUN), -1, jnp.int32), target], 1).reshape(-1)
    to_place = (jnp.arange(TOK, dtype=jnp.int32)[:, None] == target[None, :]).astype(BF)
    placed = arrived[:, : 2 * RUN].reshape(2 * TOK, WIDTH)
    cache = jnp.dot(to_place, placed, preferred_element_type=F32).astype(BF)

    own_odd = lax.dynamic_index_in_dim(slot_odd, pre_rank, 0, keepdims=False)
    own_length = lax.dynamic_index_in_dim(slot_length, pre_rank, 0, keepdims=False)
    key_residue = jnp.where(own_odd == 0, sender, sender_swapped)
    key_position = run[None, :] * REQS + key_residue[:, None]
    live = (key_position < own_length).astype(jnp.int32).reshape(1, TOK)
    fresh = lax.dynamic_index_in_dim(new_keys[0], pre_rank, 0, keepdims=False)
    fresh = jnp.pad(fresh, ((0, 16 - STEPS), (0, 0)))
    mixed = attend(arrived, fresh, live)
    mixed = lax.all_to_all(mixed.reshape(REQS, -1, LAT), "pre", 0, 0, tiled=True)
    mixed = mixed.reshape(REQS, STEPS, -1, LAT)
    attended = jnp.einsum("bshl,hlv->bshv", mixed, uv_weight, preferred_element_type=F32).astype(BF)
    return (cache[None], attended[None])


def solution(mesh):
    return jax.shard_map(
        shards,
        mesh=mesh,
        in_specs=(
            P("dec", None, "pre"),
            P("pre", None),
            P(),
            P("pre", None, None),
            P("pre", None, None),
            P("dec", None, None, "pre", None),
            P("dec", None, None, None),
            P(),
            P(),
            P("dec", None),
        ),
        out_specs=(P("dec", "pre", None), P("dec", None, None, "pre", None)),
        check_vma=False,
    )
```

```python
import functools
import math

import jax
import jax.numpy as jnp
from jax import lax
from jax.experimental import pallas as pl
from jax.experimental.pallas import tpu as pltpu
from jax.sharding import PartitionSpec as P

LAT = 512
ROPE = 64
WIDTH = LAT + ROPE
HDIM = 128
BLK = 64
TOK = 384
REQS = 16
RUN = TOK // REQS
NPG = TOK // BLK
PACK = 256
HOLD = 288
AHEAD = 3
PAIR = 2
SIDE = 4
HALF = 2
STEPS = 4

EPS = 1e-06
BF = jnp.bfloat16
F32 = jnp.float32


def project_kernel(
    len_ref, hid_ref, down_w_ref, up_ref, down_ref, wait_ref, own_ref,
    span_ref, shift_ref, turned_ref, hold_ref, wait_hold_ref, own_hold_ref, up_hold_ref,
    down_hold_ref, in_sem, out_sem, up_sem, down_sem,
):
    def load(part):
        where = pl.ds(part * PAIR * TOK, PAIR * TOK)
        return pltpu.make_async_copy(hid_ref.at[:, where], span_ref.at[:, where], in_sem.at[part])

    def go(step, lane, up):
        hold, out, sem = (
            (up_hold_ref, up_ref, up_sem) if up else (down_hold_ref, down_ref, down_sem)
        )
        return pltpu.make_async_copy(hold.at[step, lane], out.at[step, lane], sem.at[step, lane])

    keep_own = pltpu.make_async_copy(own_hold_ref, own_ref, out_sem.at[0])
    keep_wait = pltpu.make_async_copy(wait_hold_ref, wait_ref, out_sem.at[1])

    parts = REQS // PAIR
    for part in range(AHEAD):
        load(part).start()
    hold_ref[...] = jnp.zeros_like(hold_ref)
    turned_ref[...] = down_w_ref[...].astype(F32).T.astype(BF)
    shape = (REQS, 24, 256)
    offset = lax.broadcasted_iota(jnp.int32, shape, 2)
    offset = offset - lax.broadcasted_iota(jnp.int32, shape, 0)
    shift_ref[...] = offset - REQS * lax.broadcasted_iota(jnp.int32, shape, 1)

    start = 0
    for request in range(REQS):
        part = request // PAIR
        if request % PAIR == 0:
            load(part).wait()
            if part + AHEAD < parts:
                load(part + AHEAD).start()
        length = len_ref[lax.axis_index("dec"), request]
        count = lax.div(length + (REQS - 1), REQS)
        lead = lax.rem(start, 8)
        base = pl.multiple_of(start - lead, 8)

        for first, tokens, window in ((0, 256, 24), (256, 128, 16)):
            begin = request * TOK + first
            hid = span_ref[:, begin : begin + tokens]
            token = lax.broadcasted_iota(jnp.int32, hid.shape, 1)
            hid = jnp.where(token < count * REQS - first, hid, jnp.zeros((), BF))
            chosen = jnp.where(shift_ref[:, :window, :tokens] == -REQS * lead, 1.0, 0.0)
            chosen = chosen.reshape(REQS * window, tokens).astype(BF)
            rows = lax.dot_general(
                chosen, hid, (((1,), (1,)), ((), ())), preferred_element_type=F32
            )
            place = pl.ds(pl.multiple_of(base + first // REQS, 8), window)
            hold_ref[:, place, :] += rows.reshape(REQS, window, -1)

        start = start + count

    pre_rank, dec_rank = lax.axis_index("pre"), lax.axis_index("dec")
    along_y, along_z = lax.div(pre_rank, SIDE), lax.rem(pre_rank, SIDE)
    even = lax.rem(dec_rank, 2) == 0
    place, other = jnp.where(even, along_y, along_z), jnp.where(even, along_z, along_y)
    for away in (0, 1, 3, 2):
        for item in range(SIDE):
            residue = lax.rem(place + away, SIDE) * SIDE + lax.rem(other + item, SIDE)
            rows = hold_ref[residue, :PACK, :].astype(BF)
            part = lax.dot_general(
                turned_ref[...], rows, (((1,), (1,)), ((), ())), preferred_element_type=F32
            )
            late, lane = item // HALF, item % HALF
            if away == 0:
                own_hold_ref[item] = part
            elif away == 1 and late:
                up_hold_ref[1, lane] = part.astype(BF)
                go(1, lane, True).start()
            elif away == 1:
                wait_hold_ref[0, lane] = part
            elif away == 3 and late:
                wait_hold_ref[1, lane] = part
            elif away == 3:
                down_hold_ref[1, lane] = part.astype(BF)
                go(1, lane, False).start()
            elif late:
                down_hold_ref[0, lane] = part.astype(BF)
                go(0, lane, False).start()
            else:
                up_hold_ref[0, lane] = part.astype(BF)
                go(0, lane, True).start()
        if away == 0:
            keep_own.start()
        elif away == 3:
            keep_wait.start()
    keep_own.wait()
    keep_wait.wait()
    for step in range(2):
        for lane in range(HALF):
            go(step, lane, True).wait()
            go(step, lane, False).wait()


def project(lengths, hidden_t, kv_down):
    depth = hidden_t.shape[0]
    vmem = pl.BlockSpec(memory_space=pltpu.VMEM)
    pair = (2, HALF, WIDTH, PACK)
    return pl.pallas_call(
        project_kernel,
        out_shape=(
            jax.ShapeDtypeStruct(pair, BF),
            jax.ShapeDtypeStruct(pair, BF),
            jax.ShapeDtypeStruct(pair, F32),
            jax.ShapeDtypeStruct((SIDE, WIDTH, PACK), F32),
        ),
        in_specs=[
            pl.BlockSpec(memory_space=pltpu.SMEM),
            pl.BlockSpec(memory_space=pl.ANY),
            vmem,
        ],
        out_specs=(pl.BlockSpec(memory_space=pl.ANY),) * 4,
        scratch_shapes=[
            pltpu.VMEM((depth, REQS * TOK), BF),
            pltpu.VMEM((REQS, 24, 256), jnp.int32),
            pltpu.VMEM((WIDTH, depth), BF),
            pltpu.VMEM((REQS, HOLD, depth), F32),
            pltpu.VMEM(pair, F32),
            pltpu.VMEM((SIDE, WIDTH, PACK), F32),
            pltpu.VMEM(pair, BF),
            pltpu.VMEM(pair, BF),
            pltpu.SemaphoreType.DMA((REQS // PAIR,)),
            pltpu.SemaphoreType.DMA((2,)),
            pltpu.SemaphoreType.DMA((2, HALF)),
            pltpu.SemaphoreType.DMA((2, HALF)),
        ],
        compiler_params=pltpu.CompilerParams(vmem_limit_bytes=58 << 20),
        cost_estimate=pl.CostEstimate(
            flops=2 * REQS * TOK * depth * WIDTH, bytes_accessed=11 << 20, transcendentals=0
        ),
    )(lengths, hidden_t, kv_down)


def stage_kernel(share_ref, out_ref, sem):
    copy = pltpu.make_async_copy(share_ref, out_ref, sem)
    copy.start()
    copy.wait()


def stage(share):
    return pl.pallas_call(
        stage_kernel,
        out_shape=jax.ShapeDtypeStruct(share.shape, F32),
        in_specs=[pl.BlockSpec(memory_space=pl.ANY)],
        out_specs=pl.BlockSpec(memory_space=pltpu.VMEM),
        scratch_shapes=[pltpu.SemaphoreType.DMA],
        compiler_params=pltpu.CompilerParams(vmem_limit_bytes=8 << 20),
        cost_estimate=pl.CostEstimate(flops=0, bytes_accessed=5 << 20, transcendentals=0),
    )(share)


def relay_kernel(wait_ref, from_below_ref, from_above_ref, up_ref, down_ref):
    up_ref[...] = (wait_ref[0] + from_below_ref[0].astype(F32)).astype(BF)
    down_ref[...] = (wait_ref[1] + from_above_ref[0].astype(F32)).astype(BF)


def relay(wait, from_below, from_above):
    shape = jax.ShapeDtypeStruct((HALF, WIDTH, PACK), BF)
    return pl.pallas_call(
        relay_kernel,
        out_shape=(shape, shape),
        compiler_params=pltpu.CompilerParams(vmem_limit_bytes=8 << 20),
    )(wait, from_below, from_above)


def first_sum_kernel(
    own_ref, below_ref, above_ref, late_below_ref, late_above_ref, kept_ref, *out_refs
):
    for item in range(SIDE):
        lane = item % HALF
        if item < HALF:
            more = late_below_ref[lane].astype(F32) + above_ref[1, lane].astype(F32)
        else:
            more = below_ref[1, lane].astype(F32) + late_above_ref[lane].astype(F32)
        total = own_ref[item] + more
        if item == 0:
            kept_ref[...] = total
        else:
            out_refs[item - 1][...] = total.astype(BF)


def first_sum(own, below, above, late_below, late_above):
    share = (WIDTH, PACK)
    return pl.pallas_call(
        first_sum_kernel,
        out_shape=(jax.ShapeDtypeStruct(share, F32),)
        + (jax.ShapeDtypeStruct(share, BF),) * (SIDE - 1),
        compiler_params=pltpu.CompilerParams(vmem_limit_bytes=8 << 20),
    )(own, below, above, late_below, late_above)


def finish_kernel(
    kept_ref, one_ref, two_ref, three_ref, gain_ref, cosine_ref, sine_ref, valid_ref, out_ref):
    half = ROPE // 2
    valid = valid_ref[...] > 0
    total = kept_ref[...]
    for share_ref in (one_ref, two_ref, three_ref):
        total = total + share_ref[...].astype(F32)
    total = jnp.where(valid, total, 0.0)
    latent = total[:LAT]
    scaling = lax.rsqrt(jnp.sum(latent * latent, 0, keepdims=True) / LAT + EPS)
    latent = (latent * scaling * gain_ref[...]).astype(BF)
    first, second = total[LAT : LAT + half], total[LAT + half :]
    cosine, sine = cosine_ref[...], sine_ref[...]
    left = (first * cosine - second * sine).astype(BF)
    right = (second * cosine + first * sine).astype(BF)
    for copy in range(SIDE):
        out_ref[copy, :LAT] = latent
        out_ref[copy, LAT : LAT + half] = left
        out_ref[copy, LAT + half :] = right


def finish(kept, one, two, three, gain, cosine, sine, valid):
    return pl.pallas_call(
        finish_kernel,
        out_shape=jax.ShapeDtypeStruct((SIDE, WIDTH, PACK), BF),
        compiler_params=pltpu.CompilerParams(vmem_limit_bytes=24 << 20),
    )(kept, one, two, three, gain, cosine, sine, valid)


def select_kernel(source_ref, order_ref, near_ref, far_ref, query_ref, out_ref):
    row = lax.broadcasted_iota(jnp.int32, (PACK, TOK), 0)
    mine = jnp.zeros((WIDTH, TOK), F32)
    for side, rows_ref in enumerate((near_ref, far_ref)):
        for x in range(SIDE):
            target = source_ref[side : side + 1, :] - x * PACK
            chosen = jnp.where(row == target, 1.0, 0.0).astype(BF)
            mine = mine + jnp.dot(rows_ref[x], chosen, preferred_element_type=F32)
    column = lax.broadcasted_iota(jnp.int32, (2 * TOK, TOK), 1)
    order = jnp.where(column == order_ref[...], 1.0, 0.0).astype(BF)
    picked = lax.dot_general(
        order, mine.astype(BF), (((1,), (1,)), ((), ())), preferred_element_type=F32
    ).astype(BF)
    out_ref[:, : 2 * RUN] = picked.reshape(REQS, 2 * RUN, WIDTH)
    out_ref[:, 2 * RUN :] = query_ref[...]


def select(source, order, near, far, query):
    return pl.pallas_call(
        select_kernel,
        out_shape=jax.ShapeDtypeStruct((REQS, 2 * RUN + query.shape[1], WIDTH), BF),
        compiler_params=pltpu.CompilerParams(vmem_limit_bytes=40 << 20),
    )(source, order, near, far, query)


def attend_kernel(arrived_ref, fresh_ref, live_ref, out_ref):
    scale = 1.0 / math.sqrt(HDIM + ROPE)
    across = (((1,), (1,)), ((), ()))
    row = lax.broadcasted_iota(jnp.int32, (TOK, 2 * TOK), 0)
    column = lax.broadcasted_iota(jnp.int32, (TOK, 2 * TOK), 1)
    kept = jnp.where(row + RUN * lax.div(row, RUN) == column, 1.0, 0.0).astype(BF)
    rows = arrived_ref[:, : 2 * RUN].reshape(2 * TOK, WIDTH)
    keys = jnp.dot(kept, rows, preferred_element_type=F32).astype(BF)
    fresh = fresh_ref[...]
    query = arrived_ref[:, 2 * RUN :].reshape(-1, WIDTH)
    score = lax.dot_general(query, keys, across, preferred_element_type=F32) * scale
    score = jnp.where(live_ref[...] > 0, score, -1e30)
    later = lax.dot_general(query, fresh, across, preferred_element_type=F32) * scale
    row = lax.broadcasted_iota(jnp.int32, later.shape, 0)
    column = lax.broadcasted_iota(jnp.int32, later.shape, 1)
    at_step = lax.rem(lax.div(row, 8), STEPS)
    later = jnp.where(column <= at_step, later, -1e30)
    top = jnp.maximum(jnp.max(score, -1, keepdims=True), jnp.max(later, -1, keepdims=True))
    score = jnp.exp(score - top)
    later = jnp.exp(later - top)
    total = jnp.sum(score, -1, keepdims=True) + jnp.sum(later, -1, keepdims=True)
    inverse = 1.0 / total
    score = (score * inverse).astype(BF)
    later = (later * inverse).astype(BF)
    mixed = jnp.dot(score, keys[:, :LAT], preferred_element_type=F32)
    mixed = mixed + jnp.dot(later, fresh[:, :LAT], preferred_element_type=F32)
    out_ref[...] = mixed.astype(BF)


def attend(arrived, fresh, live):
    count = REQS * (arrived.shape[1] - 2 * RUN)
    return pl.pallas_call(
        attend_kernel,
        out_shape=jax.ShapeDtypeStruct((count, LAT), BF),
        compiler_params=pltpu.CompilerParams(vmem_limit_bytes=24 << 20),
    )(arrived, fresh, live)


def pick(index, values):
    ids = jnp.arange(values.shape[0], dtype=jnp.int32)
    return jnp.sum(jnp.where(index[..., None] == ids, values, 0), -1)


def neighbours(step, turn=0):
    pairs = []
    for pre in range(REQS):
        y, z = pre // SIDE, pre % SIDE
        for dec in range(2 * SIDE):
            up_y = dec % 2 == turn
            ny, nz = ((y + step) % SIDE, z) if up_y else (y, (z + step) % SIDE)
            pairs.append((pre * 2 * SIDE + dec, (ny * SIDE + nz) * 2 * SIDE + dec))
    return pairs


def shards(
    hidden, kv_down, kv_gain, uk_weight, uv_weight, queries, new_keys, lengths, assign, block_table
):
    pre_rank = lax.axis_index("pre")
    dec_rank = lax.axis_index("dec")
    both = ("pre", "dec")
    side_y, side_z = pre_rank // SIDE, pre_rank % SIDE
    swapped = side_z * SIDE + side_y
    residue = jnp.where(dec_rank % 2 == 0, pre_rank, swapped)

    counts = (lengths + (REQS - 1)) // REQS
    ends = jnp.cumsum(counts, 1)
    starts = ends - counts
    own_lengths = lax.dynamic_index_in_dim(lengths, dec_rank, 0, keepdims=False)
    own_starts = lax.dynamic_index_in_dim(starts, dec_rank, 0, keepdims=False)
    own_ends = lax.dynamic_index_in_dim(ends, dec_rank, 0, keepdims=False)

    up, down, wait, own = project(lengths, hidden[0].T, kv_down)

    below = lax.ppermute(up, both, neighbours(1))
    above = lax.ppermute(down, both, neighbours(-1))
    up, down = relay(stage(wait), below, above)
    own, up, down = lax.optimization_barrier((own, up, down))
    late_below = lax.ppermute(up, both, neighbours(1))
    late_above = lax.ppermute(down, both, neighbours(-1))
    kept, *shares = first_sum(stage(own), below, above, late_below, late_above)
    shares = [lax.ppermute(part, both, neighbours(k + 1, 1)) for k, part in enumerate(shares)]

    row = jnp.arange(PACK, dtype=jnp.int32)
    inside = (row >= own_starts[:, None]) & (row < own_ends[:, None])
    place = jnp.sum(jnp.where(inside, row - own_starts[:, None], 0), 0)
    limit = jnp.sum(jnp.where(inside, own_lengths[:, None], 0), 0)
    position = place * REQS + residue
    valid = (position < limit).astype(jnp.int32)[None, :]
    half = ROPE // 2
    frequency = 10000.0 ** (-jnp.arange(half, dtype=F32) * 2.0 / ROPE)
    angles = position[None, :].astype(F32) * frequency[:, None]
    rows = finish(kept, *shares, kv_gain[:, None], jnp.cos(angles), jnp.sin(angles), valid)

    local_queries = queries[0]
    absorbed = jnp.einsum(
        "bshk,hkl->bshl", local_queries[..., :HDIM], uk_weight, preferred_element_type=F32
    ).astype(BF)
    query_full = jnp.concatenate([absorbed, local_queries[..., HDIM:]], -1)
    query_full = query_full.reshape(REQS, -1, WIDTH)

    along_x = [[2 * x + core for x in range(SIDE)] for core in range(2)]
    near = lax.all_to_all(rows, "dec", 0, 0, tiled=True, axis_index_groups=along_x)
    far = lax.ppermute(near, "dec", [(d, d ^ 1) for d in range(2 * SIDE)])

    slots = lax.dynamic_slice_in_dim(assign, dec_rank * REQS, REQS)
    slot_start = pick(slots, (starts + jnp.arange(starts.shape[0])[:, None] // 2 * PACK).reshape(-1))
    slot_count = pick(slots, counts.reshape(-1))
    slot_length = pick(slots, lengths.reshape(-1))
    slot_odd = (slots // REQS) % 2
    run = jnp.arange(RUN, dtype=jnp.int32)
    by_slot = jnp.where(run < slot_count[:, None], slot_start[:, None] + run, -1)
    is_near = (slot_odd == dec_rank % 2)[:, None]
    source = jnp.stack([jnp.where(is_near, by_slot, -1), jnp.where(is_near, -1, by_slot)])
    table = block_table[0]
    pages = table.shape[0]
    page = jnp.arange(pages, dtype=jnp.int32)
    block = jnp.sum(jnp.where(table[None, :] == page[:, None], page[None, :], 0), 1)
    owner, part = block // NPG, block % NPG
    piece = part[:, None] * (RUN // NPG) + jnp.arange(RUN // NPG, dtype=jnp.int32)
    by_page = (owner[:, None] * RUN + piece).reshape(REQS, RUN)
    in_order = jnp.arange(TOK, dtype=jnp.int32).reshape(REQS, RUN)
    order = jnp.concatenate([in_order, by_page], 1).reshape(-1, 1)
    outgoing = select(source.reshape(2, -1), order, near, far, query_full)
    arrived = lax.all_to_all(outgoing, "pre", 0, 0, tiled=True)

    sender = jnp.arange(REQS, dtype=jnp.int32)
    sender_swapped = (sender % SIDE) * SIDE + sender // SIDE
    page_odd = pick(owner, slot_odd).reshape(REQS, NPG)
    page_odd = lax.dynamic_index_in_dim(page_odd, pre_rank, 0, keepdims=False)
    sent_residue = jnp.where(page_odd[None, :] == 0, sender[:, None], sender_swapped[:, None])
    target = (
        jnp.arange(NPG, dtype=jnp.int32)[None, :, None] * BLK
        + jnp.arange(RUN // NPG, dtype=jnp.int32)[None, None, :] * REQS
        + sent_residue[:, :, None]
    ).reshape(REQS, RUN)
    target = jnp.concatenate([jnp.full((REQS, RUN), -1, jnp.int32), target], 1).reshape(-1)
    to_place = (jnp.arange(TOK, dtype=jnp.int32)[:, None] == target[None, :]).astype(BF)
    placed = arrived[:, : 2 * RUN].reshape(2 * TOK, WIDTH)
    cache = jnp.dot(to_place, placed, preferred_element_type=F32).astype(BF)

    own_odd = lax.dynamic_index_in_dim(slot_odd, pre_rank, 0, keepdims=False)
    own_length = lax.dynamic_index_in_dim(slot_length, pre_rank, 0, keepdims=False)
    key_residue = jnp.where(own_odd == 0, sender, sender_swapped)
    key_position = run[None, :] * REQS + key_residue[:, None]
    live = (key_position < own_length).astype(jnp.int32).reshape(1, TOK)
    fresh = lax.dynamic_index_in_dim(new_keys[0], pre_rank, 0, keepdims=False)
    fresh = jnp.pad(fresh, ((0, 16 - STEPS), (0, 0)))
    mixed = attend(arrived, fresh, live)
    mixed = lax.all_to_all(mixed.reshape(REQS, -1, LAT), "pre", 0, 0, tiled=True)
    mixed = mixed.reshape(REQS, STEPS, -1, LAT)
    attended = jnp.einsum("bshl,hlv->bshv", mixed, uv_weight, preferred_element_type=F32).astype(BF)
    return (cache[None], attended[None])


def solution(mesh):
    return jax.shard_map(
        shards,
        mesh=mesh,
        in_specs=(
            P("dec", None, "pre"),
            P("pre", None),
            P(),
            P("pre", None, None),
            P("pre", None, None),
            P("dec", None, None, "pre", None),
            P("dec", None, None, None),
            P(),
            P(),
            P("dec", None),
        ),
        out_specs=(P("dec", "pre", None), P("dec", None, None, "pre", None)),
        check_vma=False,
    )
```
